32 devices in a mesh: seq: 4 (over z), head: 8 (over y, x, core).
Axes of the slice: x: 2, y: 2, z: 4, core: 2. Of those that a mesh axis runs over, the one named last changes fastest.
Arguments:
- queries: bfloat16 [1024, 8192], P('seq', 'head'), may hold values from -41 to 41
- keys: bfloat16 [4, 200, 8, 128], P('seq', 'head'), may hold values from -4 to 4
- values: bfloat16 [4, 200, 8, 128], P('seq', 'head'), may hold values from -6 to 6
- cotangent: bfloat16 [1024, 8192], P('seq', 'head'), may hold values from -6 to 6
- mask: int32 [1024, 2], P('seq'), may hold values from 0 to 1, as said below
Outputs:
- attended: bfloat16 [1024, 8192], P('seq', 'head')
- grad_query: bfloat16 [1024, 8192], P('seq', 'head')
- grad_keys: bfloat16 [4, 200, 8, 128], P('seq', 'head')
- grad_values: bfloat16 [4, 200, 8, 128], P('seq', 'head')
The draws below stay inside these ranges and needn't reach their ends.
Inputs may be any that keep to these rules, and one draw needn't show every extreme that they name: mask[t, 0] is 1 where token t attends to the image of its own block of 256 tokens, mask[t, 1] where it attends to the image of the block before. Within each block the ones of column 0 form a suffix that covers at least the block's second half, the ones of column 1 a prefix that holds the block's first token and at most its first 128 tokens, exactly that many in block 1; column 1 is all 0 on the first block.
All inputs are finite; a program needn't handle non-finite values.
Results may differ from the reference program's by a relative error of at most 0.038.
Values may be sent and summed in bfloat16 or wider, within the bound.
A program may use at most 64 MiB of HBM per device.

```python
import jax
import jax.numpy as jnp
from jax import lax

QH = 64
KVH = 8
HD = 128
TXT = 256
VTOK = 200
HPD = 8
IMAGES = 4
TOKENS = 1024
N_SEQ = 4
N_HEAD = 8


def key_field(key):
    field = jnp.clip(jax.random.normal(jax.random.fold_in(key, 5), (IMAGES, VTOK, KVH, HD), jnp.float32), -4.0, 4.0)
    return field


def draw_keys(key, part):
    raw_keys = key_field(key)
    return raw_keys.astype(jnp.bfloat16)


def draw_queries(key, part):
    field = jnp.clip(2.0 * jax.random.normal(jax.random.fold_in(key, 21), (TOKENS, QH, HD), jnp.float32), -8.0, 8.0)
    return field.reshape(TOKENS, QH * HD).astype(jnp.bfloat16)


def draw_mask(key, part):
    suffix_start = jax.random.randint(jax.random.fold_in(key, 11), (IMAGES,), 0, TXT // 2)
    prefix_end = jax.random.randint(jax.random.fold_in(key, 12), (IMAGES,), 1, TXT // 2 + 1)
    block_ids = jnp.arange(IMAGES, dtype=jnp.int32)
    prefix_end = jnp.where(block_ids == 1, TXT // 2, prefix_end)
    prefix_end = jnp.where(block_ids == 0, 0, prefix_end)
    position = jnp.arange(TXT, dtype=jnp.int32)
    own_cols = (position[None, :] >= suffix_start[:, None]).astype(jnp.int32)
    prev_cols = (position[None, :] < prefix_end[:, None]).astype(jnp.int32)
    return jnp.stack([own_cols, prev_cols], axis=-1).reshape(TOKENS, 2)


def block_scale(rng, dims, cuts, smallest, top_value):
    loudness = 1.0
    for dim, shards_of in cuts:
        heights = jax.random.uniform(jax.random.fold_in(jax.random.fold_in(rng, 6), dim), (shards_of,), jnp.float32, smallest / len(cuts), top_value / len(cuts))
        loudness = loudness * jnp.repeat(jnp.exp(heights), dims[dim] // shards_of).reshape((-1,) + (1,) * (len(dims) - 1 - dim))
    return loudness


def scatter_about(stream_key, dims, width, most, shards=(), held_as=jnp.bfloat16):
    entries = jax.random.normal(stream_key, dims, jnp.float32) * width
    if len(shards) > 0:
        entries = block_scale(stream_key, dims, shards, -0.22, 0.18) * entries
    return jnp.clip(entries, min=-most, max=most).astype(held_as)


def setup_inputs(seed: int = 0) -> dict:
    splits = jax.random.split(jax.random.key(seed), 6)
    return {
        "queries": draw_queries(jax.random.fold_in(splits[5], 71), 0),
        "keys": draw_keys(jax.random.fold_in(splits[5], 71), 0),
        "values": scatter_about(splits[2], (IMAGES, VTOK, KVH, HD), 1.0, 6.0, ((0, 4), (1, 8))),
        "cotangent": scatter_about(splits[3], (TOKENS, QH * HD), 1.0, 6.0, ((0, 4), (1, 8))),
        "mask": draw_mask(jax.random.fold_in(splits[5], 71), 0),
    }


NEGATIVE = -1e30


def bround(array):
    return lax.optimization_barrier(array.astype(jnp.bfloat16)).astype(jnp.float32)


def expand_heads(kv_block):
    return jnp.repeat(kv_block.astype(jnp.float32), QH // KVH, axis=1)


def block_forward(query_block, key_block, value_block, keep_mask):
    key_wide = expand_heads(key_block)
    value_wide = expand_heads(value_block)
    scores = jnp.einsum("thd,khd->thk", query_block, key_wide) * (HD ** -0.5)
    scores = jnp.where(keep_mask[:, None, None] > 0, scores, NEGATIVE)
    highest = jnp.max(scores, axis=2)
    powered = jnp.exp(scores - highest[:, :, None])
    totals = jnp.sum(powered, axis=2)
    partial_value = jnp.einsum("thk,khd->thd", bround(powered), value_wide)
    return scores, highest, totals, partial_value, key_wide, value_wide


def fold_heads(term):
    blocks = term.reshape(VTOK, N_HEAD, HPD, HD).sum(axis=2)
    rounded = bround(blocks)
    return rounded.reshape(VTOK, KVH, N_HEAD // KVH, HD).sum(axis=2)


def block_backward(scores, highest, totals, live_rows, grad_block, row_delta, query_block, key_wide, value_wide):
    weights = live_rows[:, :, None] * jnp.exp(scores - highest[:, :, None]) / totals[:, :, None]
    grad_weights = jnp.einsum("thd,khd->thk", grad_block, value_wide)
    grad_scores = bround(weights * (grad_weights - row_delta[:, :, None]) * (HD ** -0.5))
    grad_query = jnp.einsum("thk,khd->thd", grad_scores, key_wide)
    key_part = jnp.einsum("thk,thd->khd", grad_scores, query_block)
    value_part = jnp.einsum("thk,thd->khd", bround(weights), grad_block)
    return grad_query, fold_heads(key_part), fold_heads(value_part)


def reference(queries, keys, values, cotangent, mask):
    query_blocks = queries.reshape(N_SEQ, TXT, QH, HD)
    grad_blocks = cotangent.reshape(N_SEQ, TXT, QH, HD)
    mask_blocks = mask.reshape(N_SEQ, TXT, 2)
    prev_keys = jnp.roll(keys, 1, axis=0)
    prev_values = jnp.roll(values, 1, axis=0)

    def one_block(inputs):
        query_raw, grad_raw, mask_block, key_own, value_own, key_prev, value_prev = inputs
        query_block = query_raw.astype(jnp.float32)
        grad_block = grad_raw.astype(jnp.float32)
        score_own, peak_own, total_own, partial_own, keyw_own, valw_own = block_forward(query_block, key_own, value_own, mask_block[:, 0])
        score_prev, peak_prev, total_prev, partial_prev, keyw_prev, valw_prev = block_forward(query_block, key_prev, value_prev, mask_block[:, 1])
        highest = jnp.maximum(peak_own, peak_prev)
        scale_own = jnp.exp(peak_own - highest)
        scale_prev = jnp.exp(peak_prev - highest)
        totals = scale_own * total_own + scale_prev * total_prev
        live_rows = ((mask_block[:, 0] + mask_block[:, 1]) > 0).astype(jnp.float32)[:, None]
        attended = (live_rows[:, :, None] * (scale_own[:, :, None] * partial_own + scale_prev[:, :, None] * partial_prev) / totals[:, :, None]).astype(jnp.bfloat16)
        row_delta = jnp.sum(grad_block * attended.astype(jnp.float32), axis=2)
        gq_own, gk_own, gv_own = block_backward(score_own, highest, totals, live_rows, grad_block, row_delta, query_block, keyw_own, valw_own)
        gq_prev, gk_prev, gv_prev = block_backward(score_prev, highest, totals, live_rows, grad_block, row_delta, query_block, keyw_prev, valw_prev)
        grad_query = (gq_own + gq_prev).astype(jnp.bfloat16)
        return attended, grad_query, gk_own, gv_own, gk_prev, gv_prev

    outputs = lax.map(one_block, (query_blocks, grad_blocks, mask_blocks, keys, values, prev_keys, prev_values))
    attended = outputs[0].reshape(TOKENS, QH * HD)
    grad_query = outputs[1].reshape(TOKENS, QH * HD)
    padding = jnp.zeros((1, VTOK, KVH, HD), jnp.float32)
    key_next = jnp.concatenate([outputs[4][1:], padding], axis=0)
    value_next = jnp.concatenate([outputs[5][1:], padding], axis=0)
    grad_keys = (outputs[2] + key_next).astype(jnp.bfloat16)
    grad_values = (outputs[3] + value_next).astype(jnp.bfloat16)
    return attended, grad_query, grad_keys, grad_values
```

```python
import functools
import math

import jax
import jax.numpy as jnp
from jax import lax
from jax.experimental import pallas as pl
from jax.experimental.pallas import tpu as pltpu
from jax.sharding import PartitionSpec as P

KVH = 8
HD = 128
NEGATIVE = -1e30
MESH = pl.DeviceIdType.MESH
SCALE = HD ** -0.5
EXP2_SCALE = SCALE * math.log2(math.e)


def dot(a, b):
    return jnp.dot(a, b, preferred_element_type=jnp.float32)


def dot_nt(a, b):
    return lax.dot_general(a, b, (((1,), (1,)), ((), ())), preferred_element_type=jnp.float32)


def each(count, body):
    if count <= 8:
        for i in range(count):
            body(i)
    else:
        lax.fori_loop(0, count, lambda i, c: (body(i), c)[1], 0)


def slot_map(pad, vision, transposed):
    shape = (vision * KVH, KVH * pad) if transposed else (KVH * pad, vision * KVH)
    slot = lax.broadcasted_iota(jnp.int32, shape, 1 if transposed else 0)
    row = lax.broadcasted_iota(jnp.int32, shape, 0 if transposed else 1)
    head, token = slot // pad, slot % pad
    return jnp.where((token < vision) & (row == token * KVH + head), 1.0, 0.0).astype(jnp.bfloat16)


def kernel(
    n_seq, n, pad, vision, group,
    q_hbm, k_ref, v_ref, do_hbm, mask_ref,
    att_hbm, gq_hbm, gk_ref, gv_ref,
    q, do, att, gq, qt, dot_t, stage, kv, part, ret, bias,
    in_sem, out_sem, kv_send, kv_recv, part_send, part_recv,
):
    s = lax.axis_index("seq")
    me = lax.axis_index("head")
    copies = n // KVH
    tokens, width = q.shape
    heads = width // HD
    half = tokens // 2
    cols = n * pad
    not_first = s > 0
    not_last = s < n_seq - 1

    loads = []
    for i, rows in enumerate((pl.ds(half, half), pl.ds(0, half))):
        for k, (src, dst) in enumerate(((q_hbm, q), (do_hbm, do))):
            load = pltpu.make_async_copy(src.at[rows], dst.at[rows], in_sem.at[i, k])
            load.start()
            loads.append(load)

    barrier = pltpu.get_barrier_semaphore()

    def greet(block, peer):
        pl.semaphore_signal(
            barrier, inc=1, device_id={"seq": block, "head": peer}, device_id_type=MESH
        )

    each(n - 1, lambda i: greet(s, lax.rem(me + 1 + i, n)))

    @pl.when(not_first)
    def _():
        each(n, lambda i: greet(s - 1, lax.rem(me + i, n)))

    @pl.when(not_last)
    def _():
        each(n, lambda i: greet(s + 1, lax.rem(me + i, n)))

    spread = slot_map(pad, vision, False)
    stage[:, :HD] = dot(spread, k_ref[...]).astype(jnp.bfloat16)
    stage[:, HD:] = dot(spread, v_ref[...]).astype(jnp.bfloat16)

    def rows_of(index):
        return pl.ds(pl.multiple_of(index * pad, pad), pad)

    def kv_copy(b, block, peer, source):
        return pltpu.make_async_remote_copy(
            src_ref=stage.at[rows_of(peer // copies)],
            dst_ref=kv.at[b, rows_of(source)],
            send_sem=kv_send.at[b, peer],
            recv_sem=kv_recv.at[b, source],
            device_id={"seq": block, "head": peer},
            device_id_type=MESH,
        )

    def part_copy(b, block, peer, source):
        return pltpu.make_async_remote_copy(
            src_ref=part.at[b, rows_of(peer)],
            dst_ref=ret.at[b, rows_of(source)],
            send_sem=part_send.at[b, peer],
            recv_sem=part_recv.at[b, source],
            device_id={"seq": block, "head": peer},
            device_id_type=MESH,
        )

    pl.semaphore_wait(
        barrier, (n - 1) + n * not_first.astype(jnp.int32) + n * not_last.astype(jnp.int32)
    )

    each(n - 1, lambda i: kv_copy(0, s, lax.rem(me + 1 + i, n), me).start())

    @pl.when(not_last)
    def _():
        each(n, lambda i: kv_copy(1, s + 1, lax.rem(me + i, n), me).start())

    kv[0, rows_of(me), :] = stage[rows_of(me // copies), :]

    @pl.when(s == 0)
    def _():
        kv[1] = jnp.zeros(kv.shape[1:], kv.dtype)

    @pl.when(s == n_seq - 1)
    def _():
        ret[1] = jnp.zeros(ret.shape[1:], ret.dtype)

    slot_col = lax.broadcasted_iota(jnp.int32, (half, cols), 1)
    used = slot_col % pad < vision
    keep_own = mask_ref[:half, 0:1]
    keep_prev = mask_ref[:half, 1:2]
    bias[:, :cols] = jnp.where(used & (keep_own > 0), 0.0, NEGATIVE)
    bias[:, cols:] = jnp.where(used & (keep_prev > 0), 0.0, NEGATIVE)
    live = (keep_own + keep_prev > 0).astype(jnp.float32)
    live = jnp.concatenate([live] * group, axis=0)
    own_bias = jnp.where(used[:1], 0.0, NEGATIVE)

    for load in loads:
        load.wait()
    for h in range(heads):
        at = slice(h * HD, (h + 1) * HD)
        for b in range(2):
            to = slice(h * half, (h + 1) * half)
            rows = slice(b * half, (b + 1) * half)
            qt[b, :, to] = q[rows, at].T
            dot_t[b, :, to] = do[rows, at].T

    def stacked(ref, rows, first):
        return jnp.concatenate(
            [ref[rows, (first + i) * HD:(first + i + 1) * HD] for i in range(group)], axis=0
        )

    def attend(rows, b, first, keys, values, score_bias, live_rows):
        query = stacked(q, rows, first)
        grad = stacked(do, rows, first)
        scores = dot_nt(query, keys) + score_bias
        peak = jnp.max(scores, axis=1, keepdims=True)
        powered = jnp.exp2((scores - peak) * EXP2_SCALE)
        weights = powered * (live_rows / jnp.sum(powered, axis=1, keepdims=True))
        rounded = weights.astype(jnp.bfloat16)
        attended = dot(rounded, values)
        delta = jnp.sum(grad.astype(jnp.float32) * attended, axis=1, keepdims=True)
        grad_weights = dot_nt(grad, values)
        grad_scores = (weights * (grad_weights - delta)).astype(jnp.bfloat16)
        grad_query = dot(grad_scores, keys) * SCALE
        for i in range(group):
            at = slice((first + i) * HD, (first + i + 1) * HD)
            att[rows, at] = attended[i * half:(i + 1) * half].astype(jnp.bfloat16)
            gq[rows, at] = grad_query[i * half:(i + 1) * half].astype(jnp.bfloat16)
        to = slice(first * half, (first + group) * half)
        return dot(qt[b, :, to], grad_scores), dot(dot_t[b, :, to], rounded)

    def put(b, key_sum, value_sum):
        part[b, :, :HD] = (key_sum * SCALE).T.astype(jnp.bfloat16)
        part[b, :, HD:] = value_sum.T.astype(jnp.bfloat16)

    def write_out(b):
        rows = pl.ds(b * half, half)
        stores = [
            pltpu.make_async_copy(att.at[rows], att_hbm.at[rows], out_sem.at[b, 0]),
            pltpu.make_async_copy(gq.at[rows], gq_hbm.at[rows], out_sem.at[b, 1]),
        ]
        for store in stores:
            store.start()
        return stores

    upper, lower = slice(half, tokens), slice(0, half)
    firsts = list(range(0, heads, group))
    cut = len(firsts) // 2

    each(n - 1, lambda i: kv_copy(0, s, me, lax.rem(me + 1 + i, n)).wait_recv())
    key_sum, value_sum = 0.0, 0.0
    keys, values = kv[0, :, :HD], kv[0, :, HD:]
    for first in firsts[:cut]:
        key_term, value_term = attend(upper, 1, first, keys, values, own_bias, 1.0)
        key_sum, value_sum = key_sum + key_term, value_sum + value_term

    @pl.when(not_first)
    def _():
        each(n, lambda i: kv_copy(1, s, me, lax.rem(me + i, n)).wait_recv())

    both_keys = kv[:, :, :HD].reshape(2 * cols, HD)
    both_values = kv[:, :, HD:].reshape(2 * cols, HD)
    both_bias = jnp.concatenate([bias[...]] * group, axis=0)
    key_both, value_both = 0.0, 0.0
    for first in firsts:
        key_term, value_term = attend(lower, 0, first, both_keys, both_values, both_bias, live)
        key_both, value_both = key_both + key_term, value_both + value_term
    put(1, key_both[:, cols:], value_both[:, cols:])

    @pl.when(not_first)
    def _():
        each(n, lambda i: part_copy(1, s - 1, lax.rem(me + i, n), me).start())

    stores = write_out(0)
    key_sum, value_sum = key_sum + key_both[:, :cols], value_sum + value_both[:, :cols]
    for first in firsts[cut:]:
        key_term, value_term = attend(upper, 1, first, keys, values, own_bias, 1.0)
        key_sum, value_sum = key_sum + key_term, value_sum + value_term
    put(0, key_sum, value_sum)
    each(n - 1, lambda i: part_copy(0, s, lax.rem(me + 1 + i, n), me).start())
    stores += write_out(1)
    ret[0, rows_of(me), :] = part[0, rows_of(me), :]

    gather = slot_map(pad, vision, True)
    each(n - 1, lambda i: part_copy(0, s, me, lax.rem(me + 1 + i, n)).wait_recv())

    @pl.when(not_last)
    def _():
        each(n, lambda i: part_copy(1, s, me, lax.rem(me + i, n)).wait_recv())

    total = ret[0].astype(jnp.float32) + ret[1].astype(jnp.float32)
    total = total.reshape(KVH, copies, pad, 2 * HD).sum(axis=1).reshape(KVH * pad, 2 * HD)
    grads = dot(gather, total.astype(jnp.bfloat16)).astype(jnp.bfloat16)
    gk_ref[...] = grads[:, :HD]
    gv_ref[...] = grads[:, HD:]

    each(n - 1, lambda i: kv_copy(0, s, lax.rem(me + 1 + i, n), me).wait_send())
    each(n - 1, lambda i: part_copy(0, s, lax.rem(me + 1 + i, n), me).wait_send())

    @pl.when(not_last)
    def _():
        each(n, lambda i: kv_copy(1, s + 1, lax.rem(me + i, n), me).wait_send())

    @pl.when(not_first)
    def _():
        each(n, lambda i: part_copy(1, s - 1, lax.rem(me + i, n), me).wait_send())

    for store in stores:
        store.wait()


def per_device(n_seq, n, queries, keys, values, cotangent, mask):
    tokens, width = queries.shape
    vision = keys.shape[1]
    pad = -(-vision // 16) * 16
    heads = width // HD
    group = min(2, heads)
    half = tokens // 2
    cols = n * pad
    bf16, f32 = jnp.bfloat16, jnp.float32
    vmem = pl.BlockSpec(memory_space=pltpu.VMEM)
    hbm = pl.BlockSpec(memory_space=pl.ANY)
    dma = pltpu.SemaphoreType.DMA
    attended, grad_query, grad_keys, grad_values = pl.pallas_call(
        functools.partial(kernel, n_seq, n, pad, vision, group),
        out_shape=(
            jax.ShapeDtypeStruct((tokens, width), bf16),
            jax.ShapeDtypeStruct((tokens, width), bf16),
            jax.ShapeDtypeStruct((vision * KVH, HD), bf16),
            jax.ShapeDtypeStruct((vision * KVH, HD), bf16),
        ),
        in_specs=[hbm, vmem, vmem, hbm, vmem],
        out_specs=(hbm, hbm, vmem, vmem),
        scratch_shapes=[
            pltpu.VMEM((tokens, width), bf16),
            pltpu.VMEM((tokens, width), bf16),
            pltpu.VMEM((tokens, width), bf16),
            pltpu.VMEM((tokens, width), bf16),
            pltpu.VMEM((2, HD, heads * half), bf16),
            pltpu.VMEM((2, HD, heads * half), bf16),
            pltpu.VMEM((KVH * pad, 2 * HD), bf16),
            pltpu.VMEM((2, cols, 2 * HD), bf16),
            pltpu.VMEM((2, cols, 2 * HD), bf16),
            pltpu.VMEM((2, cols, 2 * HD), bf16),
            pltpu.VMEM((half, 2 * cols), f32),
            dma((2, 2)),
            dma((2, 2)),
            dma((2, n)),
            dma((2, n)),
            dma((2, n)),
            dma((2, n)),
        ],
        compiler_params=pltpu.CompilerParams(
            collective_id=0, has_side_effects=True, vmem_limit_bytes=48 * 1024 * 1024
        ),
    )(
        queries,
        keys.reshape(vision * KVH, HD),
        values.reshape(vision * KVH, HD),
        cotangent,
        mask,
    )
    shape = (1, vision, KVH, HD)
    return attended, grad_query, grad_keys.reshape(shape), grad_values.reshape(shape)


def solution(mesh):
    return jax.shard_map(
        functools.partial(per_device, mesh.shape["seq"], mesh.shape["head"]),
        mesh=mesh,
        in_specs=(
            P("seq", "head"),
            P("seq", "head", None, None),
            P("seq", "head", None, None),
            P("seq", "head"),
            P("seq", None),
        ),
        out_specs=(
            P("seq", "head"),
            P("seq", "head"),
            P("seq", "head", None, None),
            P("seq", "head", None, None),
        ),
        check_vma=False,
    )
```

```python
import functools
import math

import jax
import jax.numpy as jnp
from jax import lax
from jax.experimental import pallas as pl
from jax.experimental.pallas import tpu as pltpu
from jax.sharding import PartitionSpec as P

KVH = 8
HD = 128
NEGATIVE = -1e30
VMEM_LIMIT = 58 * 1024 * 1024
MESH = pl.DeviceIdType.MESH
SCALE = HD ** -0.5
EXP2_SCALE = SCALE * math.log2(math.e)


def dot(a, b):
    return jnp.dot(a, b, preferred_element_type=jnp.float32)


def dot_nt(a, b):
    return lax.dot_general(a, b, (((1,), (1,)), ((), ())), preferred_element_type=jnp.float32)


def each(count, body):
    if count <= 8:
        for i in range(count):
            body(i)
    else:
        lax.fori_loop(0, count, lambda i, c: (body(i), c)[1], 0)


def slot_map(pad, vision, transposed):
    shape = (vision * KVH, KVH * pad) if transposed else (KVH * pad, vision * KVH)
    slot = lax.broadcasted_iota(jnp.int32, shape, 1 if transposed else 0)
    row = lax.broadcasted_iota(jnp.int32, shape, 0 if transposed else 1)
    head, token = slot // pad, slot % pad
    return jnp.where((token < vision) & (row == token * KVH + head), 1.0, 0.0).astype(jnp.bfloat16)


def kernel(
    n_seq, n, pad, vision, group,
    q_hbm, k_hbm, v_hbm, do_hbm, mask_hbm,
    att_hbm, gq_hbm, gk_ref, gv_ref,
    q, do, att, gq, k_own, v_own, mask, qt, dot_t, stage, kv, part, ret, bias, gs_lower, gs_upper,
    in_sem, out_sem, small_sem, kv_send, kv_recv, part_send, part_recv,
):
    s = lax.axis_index("seq")
    me = lax.axis_index("head")
    copies = n // KVH
    tokens, width = q.shape
    heads = width // HD
    half = tokens // 2
    cols = n * pad
    not_first = s > 0
    not_last = s < n_seq - 1

    small = []
    for i, (src, dst) in enumerate(((k_hbm, k_own), (v_hbm, v_own), (mask_hbm, mask))):
        load = pltpu.make_async_copy(src, dst, small_sem.at[i])
        load.start()
        small.append(load)
    loads = []
    for i, rows in enumerate((pl.ds(half, half), pl.ds(0, half))):
        for k, (src, dst) in enumerate(((q_hbm, q), (do_hbm, do))):
            load = pltpu.make_async_copy(src.at[rows], dst.at[rows], in_sem.at[i, k])
            load.start()
            loads.append(load)

    barrier = pltpu.get_barrier_semaphore()

    def greet(block, peer):
        pl.semaphore_signal(
            barrier, inc=1, device_id={"seq": block, "head": peer}, device_id_type=MESH
        )

    each(n - 1, lambda i: greet(s, lax.rem(me + 1 + i, n)))

    @pl.when(not_first)
    def _():
        each(n, lambda i: greet(s - 1, lax.rem(me + i, n)))

    @pl.when(not_last)
    def _():
        each(n, lambda i: greet(s + 1, lax.rem(me + i, n)))

    for load in small:
        load.wait()
    spread = slot_map(pad, vision, False)
    stage[:, :HD] = dot(spread, k_own[...]).astype(jnp.bfloat16)
    stage[:, HD:] = dot(spread, v_own[...]).astype(jnp.bfloat16)

    def rows_of(index):
        return pl.ds(pl.multiple_of(index * pad, pad), pad)

    def kv_copy(b, block, peer, source):
        return pltpu.make_async_remote_copy(
            src_ref=stage.at[rows_of(peer // copies)],
            dst_ref=kv.at[b, rows_of(source)],
            send_sem=kv_send.at[b, peer],
            recv_sem=kv_recv.at[b, source],
            device_id={"seq": block, "head": peer},
            device_id_type=MESH,
        )

    def part_copy(b, block, peer, source):
        return pltpu.make_async_remote_copy(
            src_ref=part.at[b, rows_of(peer)],
            dst_ref=ret.at[b, rows_of(source)],
            send_sem=part_send.at[b, peer],
            recv_sem=part_recv.at[b, source],
            device_id={"seq": block, "head": peer},
            device_id_type=MESH,
        )

    pl.semaphore_wait(
        barrier, (n - 1) + n * not_first.astype(jnp.int32) + n * not_last.astype(jnp.int32)
    )

    each(n - 1, lambda i: kv_copy(0, s, lax.rem(me + 1 + i, n), me).start())

    @pl.when(not_last)
    def _():
        each(n, lambda i: kv_copy(1, s + 1, lax.rem(me + i, n), me).start())

    kv[0, rows_of(me), :] = stage[rows_of(me // copies), :]

    @pl.when(s == 0)
    def _():
        kv[1] = jnp.zeros(kv.shape[1:], kv.dtype)

    @pl.when(s == n_seq - 1)
    def _():
        ret[1] = jnp.zeros(ret.shape[1:], ret.dtype)

    slot_col = lax.broadcasted_iota(jnp.int32, (half, cols), 1)
    used = slot_col % pad < vision
    columns = jnp.concatenate(
        [jnp.broadcast_to(mask[i:i + 1, :half].astype(jnp.float32), (HD, half)) for i in range(2)],
        axis=0,
    ).T
    keep_own, keep_prev = columns[:, :1], columns[:, HD:HD + 1]
    bias[:, :cols] = jnp.where(used & (keep_own > 0), 0.0, NEGATIVE)
    bias[:, cols:] = jnp.where(used & (keep_prev > 0), 0.0, NEGATIVE)
    live = (keep_own + keep_prev > 0).astype(jnp.float32)
    live = jnp.concatenate([live] * group, axis=0)
    own_bias = jnp.where(used[:1], 0.0, NEGATIVE)

    for load in loads:
        load.wait()
    for h in range(heads):
        at = slice(h * HD, (h + 1) * HD)
        for b in range(2):
            to = slice(h * half, (h + 1) * half)
            rows = slice(b * half, (b + 1) * half)
            qt[b, :, to] = q[rows, at].T
            dot_t[b, :, to] = do[rows, at].T

    def stacked(ref, rows, first):
        return jnp.concatenate(
            [ref[rows, (first + i) * HD:(first + i + 1) * HD] for i in range(group)], axis=0
        )

    def attend(rows, b, first, keys, values, score_bias, live_rows, grad_store):
        query = stacked(q, rows, first)
        grad = stacked(do, rows, first)
        scores = dot_nt(query, keys) + score_bias
        peak = jnp.max(scores, axis=1, keepdims=True)
        powered = jnp.exp2((scores - peak) * EXP2_SCALE)
        weights = powered * (live_rows / jnp.sum(powered, axis=1, keepdims=True))
        rounded = weights.astype(jnp.bfloat16)
        attended = dot(rounded, values)
        delta = jnp.sum(grad.astype(jnp.float32) * attended, axis=1, keepdims=True)
        grad_weights = dot_nt(grad, values)
        grad_scores = (weights * (grad_weights - delta)).astype(jnp.bfloat16)
        for i in range(group):
            at = slice((first + i) * HD, (first + i + 1) * HD)
            att[rows, at] = attended[i * half:(i + 1) * half].astype(jnp.bfloat16)
        to = slice(first * half, (first + group) * half)
        grad_store[to, :] = grad_scores
        return dot(qt[b, :, to], grad_scores), dot(dot_t[b, :, to], rounded)

    def put(b, key_sum, value_sum):
        part[b, :, :HD] = (key_sum * SCALE).T.astype(jnp.bfloat16)
        part[b, :, HD:] = value_sum.T.astype(jnp.bfloat16)

    def query_grads(rows, grad_store, keys):
        for first in firsts:
            grads = dot(grad_store[first * half:(first + group) * half, :], keys) * SCALE
            for i in range(group):
                at = slice((first + i) * HD, (first + i + 1) * HD)
                gq[rows, at] = grads[i * half:(i + 1) * half].astype(jnp.bfloat16)

    stores = []

    def write_out(src, dst, b, k):
        rows = pl.ds(b * half, half)
        store = pltpu.make_async_copy(src.at[rows], dst.at[rows], out_sem.at[b, k])
        store.start()
        stores.append(store)

    upper, lower = slice(half, tokens), slice(0, half)
    firsts = list(range(0, heads, group))
    cut = len(firsts) // 2

    each(n - 1, lambda i: kv_copy(0, s, me, lax.rem(me + 1 + i, n)).wait_recv())
    key_sum, value_sum = 0.0, 0.0
    keys, values = kv[0, :, :HD], kv[0, :, HD:]
    for first in firsts[:cut]:
        key_term, value_term = attend(upper, 1, first, keys, values, own_bias, 1.0, gs_upper)
        key_sum, value_sum = key_sum + key_term, value_sum + value_term

    @pl.when(not_first)
    def _():
        each(n, lambda i: kv_copy(1, s, me, lax.rem(me + i, n)).wait_recv())

    both_keys = kv[:, :, :HD].reshape(2 * cols, HD)
    both_values = kv[:, :, HD:].reshape(2 * cols, HD)
    both_bias = jnp.concatenate([bias[...]] * group, axis=0)
    key_both, value_both = 0.0, 0.0
    for first in firsts:
        key_term, value_term = attend(
            lower, 0, first, both_keys, both_values, both_bias, live, gs_lower
        )
        key_both, value_both = key_both + key_term, value_both + value_term
    put(1, key_both[:, cols:], value_both[:, cols:])

    @pl.when(not_first)
    def _():
        each(n, lambda i: part_copy(1, s - 1, lax.rem(me + i, n), me).start())

    write_out(att, att_hbm, 0, 0)
    key_sum, value_sum = key_sum + key_both[:, :cols], value_sum + value_both[:, :cols]
    for first in firsts[cut:]:
        key_term, value_term = attend(upper, 1, first, keys, values, own_bias, 1.0, gs_upper)
        key_sum, value_sum = key_sum + key_term, value_sum + value_term
    put(0, key_sum, value_sum)
    each(n - 1, lambda i: part_copy(0, s, lax.rem(me + 1 + i, n), me).start())
    ret[0, rows_of(me), :] = part[0, rows_of(me), :]
    write_out(att, att_hbm, 1, 0)
    query_grads(upper, gs_upper, keys)
    write_out(gq, gq_hbm, 1, 1)
    query_grads(lower, gs_lower, both_keys)
    write_out(gq, gq_hbm, 0, 1)

    gather = slot_map(pad, vision, True)
    each(n - 1, lambda i: part_copy(0, s, me, lax.rem(me + 1 + i, n)).wait_recv())

    @pl.when(not_last)
    def _():
        each(n, lambda i: part_copy(1, s, me, lax.rem(me + i, n)).wait_recv())

    total = ret[0].astype(jnp.float32) + ret[1].astype(jnp.float32)
    total = total.reshape(KVH, copies, pad, 2 * HD).sum(axis=1).reshape(KVH * pad, 2 * HD)
    grads = dot(gather, total.astype(jnp.bfloat16)).astype(jnp.bfloat16)
    gk_ref[...] = grads[:, :HD]
    gv_ref[...] = grads[:, HD:]

    each(n - 1, lambda i: kv_copy(0, s, lax.rem(me + 1 + i, n), me).wait_send())
    each(n - 1, lambda i: part_copy(0, s, lax.rem(me + 1 + i, n), me).wait_send())

    @pl.when(not_last)
    def _():
        each(n, lambda i: kv_copy(1, s + 1, lax.rem(me + i, n), me).wait_send())

    @pl.when(not_first)
    def _():
        each(n, lambda i: part_copy(1, s - 1, lax.rem(me + i, n), me).wait_send())

    for store in stores:
        store.wait()


def copy_out(*refs):
    count = len(refs) // 2
    copies = [pltpu.make_async_copy(refs[i], refs[count + i], refs[-1].at[i]) for i in range(count)]
    for copy in copies:
        copy.start()
    for copy in copies:
        copy.wait()


def per_device(n_seq, n, queries, keys, values, cotangent, mask):
    tokens, width = queries.shape
    vision = keys.shape[1]
    pad = -(-vision // 16) * 16
    heads = width // HD
    group = min(2, heads)
    half = tokens // 2
    cols = n * pad
    bf16, f32 = jnp.bfloat16, jnp.float32
    vmem = pl.BlockSpec(memory_space=pltpu.VMEM)
    hbm = pl.BlockSpec(memory_space=pltpu.HBM)
    anywhere = pl.BlockSpec(memory_space=pl.ANY)
    dma = pltpu.SemaphoreType.DMA
    results = (
        jax.ShapeDtypeStruct((tokens, width), bf16),
        jax.ShapeDtypeStruct((tokens, width), bf16),
        jax.ShapeDtypeStruct((vision * KVH, HD), bf16),
        jax.ShapeDtypeStruct((vision * KVH, HD), bf16),
    )
    found = pl.pallas_call(
        functools.partial(kernel, n_seq, n, pad, vision, group),
        out_shape=results,
        in_specs=[hbm] * 5,
        out_specs=(hbm, hbm, vmem, vmem),
        scratch_shapes=[
            pltpu.VMEM((tokens, width), bf16),
            pltpu.VMEM((tokens, width), bf16),
            pltpu.VMEM((tokens, width), bf16),
            pltpu.VMEM((tokens, width), bf16),
            pltpu.VMEM((vision * KVH, HD), bf16),
            pltpu.VMEM((vision * KVH, HD), bf16),
            pltpu.VMEM((2, tokens), mask.dtype),
            pltpu.VMEM((2, HD, heads * half), bf16),
            pltpu.VMEM((2, HD, heads * half), bf16),
            pltpu.VMEM((KVH * pad, 2 * HD), bf16),
            pltpu.VMEM((2, cols, 2 * HD), bf16),
            pltpu.VMEM((2, cols, 2 * HD), bf16),
            pltpu.VMEM((2, cols, 2 * HD), bf16),
            pltpu.VMEM((half, 2 * cols), f32),
            pltpu.VMEM((heads * half, 2 * cols), bf16),
            pltpu.VMEM((heads * half, cols), bf16),
            dma((2, 2)),
            dma((2, 2)),
            dma((3,)),
            dma((2, n)),
            dma((2, n)),
            dma((2, n)),
            dma((2, n)),
        ],
        compiler_params=pltpu.CompilerParams(
            collective_id=0, has_side_effects=True, vmem_limit_bytes=VMEM_LIMIT
        ),
    )(
        queries,
        keys.reshape(vision * KVH, HD),
        values.reshape(vision * KVH, HD),
        cotangent,
        mask.T,
    )
    attended, grad_query, grad_keys, grad_values = pl.pallas_call(
        copy_out,
        out_shape=results,
        in_specs=[anywhere] * 4,
        out_specs=(hbm,) * 4,
        scratch_shapes=[dma((4,))],
        compiler_params=pltpu.CompilerParams(vmem_limit_bytes=VMEM_LIMIT),
    )(*found)
    shape = (1, vision, KVH, HD)
    return attended, grad_query, grad_keys.reshape(shape), grad_values.reshape(shape)


def solution(mesh):
    return jax.shard_map(
        functools.partial(per_device, mesh.shape["seq"], mesh.shape["head"]),
        mesh=mesh,
        in_specs=(
            P("seq", "head"),
            P("seq", "head", None, None),
            P("seq", "head", None, None),
            P("seq", "head"),
            P("seq", None),
        ),
        out_specs=(
            P("seq", "head"),
            P("seq", "head"),
            P("seq", "head", None, None),
            P("seq", "head", None, None),
        ),
        check_vma=False,
    )
```

```python
import functools
import math

import jax
import jax.numpy as jnp
from jax import lax
from jax.experimental import pallas as pl
from jax.experimental.pallas import tpu as pltpu
from jax.sharding import PartitionSpec as P

KVH = 8
HD = 128
NEGATIVE = -1e30
VMEM_LIMIT = 53760 * 1024
MESH = pl.DeviceIdType.MESH
SCALE = HD ** -0.5
EXP2_SCALE = SCALE * math.log2(math.e)


def dot(a, b):
    return jnp.dot(a, b, preferred_element_type=jnp.float32)


def dot_nt(a, b):
    return lax.dot_general(a, b, (((1,), (1,)), ((), ())), preferred_element_type=jnp.float32)


def each(count, body):
    if count <= 8:
        for i in range(count):
            body(i)
    else:
        lax.fori_loop(0, count, lambda i, c: (body(i), c)[1], 0)


def slot_map(pad, vision, transposed):
    shape = (vision * KVH, KVH * pad) if transposed else (KVH * pad, vision * KVH)
    slot = lax.broadcasted_iota(jnp.int32, shape, 1 if transposed else 0)
    row = lax.broadcasted_iota(jnp.int32, shape, 0 if transposed else 1)
    head, token = slot // pad, slot % pad
    return jnp.where((token < vision) & (row == token * KVH + head), 1.0, 0.0).astype(jnp.bfloat16)


def kernel(
    n_seq, n, pad, vision, group,
    q_hbm, k_hbm, v_hbm, do_hbm, mask_hbm,
    att, gq, gk_ref, gv_ref,
    q, do, k_own, v_own, mask, qt, dot_t, stage, kv, part, ret, bias, gs_lower, gs_upper,
    in_sem, small_sem, kv_send, kv_recv, part_send, part_recv,
):
    s = lax.axis_index("seq")
    me = lax.axis_index("head")
    copies = n // KVH
    tokens, width = q.shape
    heads = width // HD
    half = tokens // 2
    cols = n * pad
    not_first = s > 0
    not_last = s < n_seq - 1

    small = []
    for i, (src, dst) in enumerate(((k_hbm, k_own), (v_hbm, v_own), (mask_hbm, mask))):
        load = pltpu.make_async_copy(src, dst, small_sem.at[i])
        load.start()
        small.append(load)
    loads = []
    for i, rows in enumerate((pl.ds(half, half), pl.ds(0, half))):
        for k, (src, dst) in enumerate(((q_hbm, q), (do_hbm, do))):
            load = pltpu.make_async_copy(src.at[rows], dst.at[rows], in_sem.at[i, k])
            load.start()
            loads.append(load)

    barrier = pltpu.get_barrier_semaphore()

    def greet(block, peer):
        pl.semaphore_signal(
            barrier, inc=1, device_id={"seq": block, "head": peer}, device_id_type=MESH
        )

    each(n - 1, lambda i: greet(s, lax.rem(me + 1 + i, n)))

    @pl.when(not_first)
    def _():
        each(n, lambda i: greet(s - 1, lax.rem(me + i, n)))

    @pl.when(not_last)
    def _():
        each(n, lambda i: greet(s + 1, lax.rem(me + i, n)))

    for load in small:
        load.wait()
    spread = slot_map(pad, vision, False)
    stage[:, :HD] = dot(spread, k_own[...]).astype(jnp.bfloat16)
    stage[:, HD:] = dot(spread, v_own[...]).astype(jnp.bfloat16)

    def rows_of(index):
        return pl.ds(pl.multiple_of(index * pad, pad), pad)

    def kv_copy(b, block, peer, source):
        return pltpu.make_async_remote_copy(
            src_ref=stage.at[rows_of(peer // copies)],
            dst_ref=kv.at[b, rows_of(source)],
            send_sem=kv_send.at[b, peer],
            recv_sem=kv_recv.at[b, source],
            device_id={"seq": block, "head": peer},
            device_id_type=MESH,
        )

    def part_copy(b, block, peer, source):
        return pltpu.make_async_remote_copy(
            src_ref=part.at[b, rows_of(peer)],
            dst_ref=ret.at[b, rows_of(source)],
            send_sem=part_send.at[b, peer],
            recv_sem=part_recv.at[b, source],
            device_id={"seq": block, "head": peer},
            device_id_type=MESH,
        )

    pl.semaphore_wait(
        barrier, (n - 1) + n * not_first.astype(jnp.int32) + n * not_last.astype(jnp.int32)
    )

    each(n - 1, lambda i: kv_copy(0, s, lax.rem(me + 1 + i, n), me).start())

    @pl.when(not_last)
    def _():
        each(n, lambda i: kv_copy(1, s + 1, lax.rem(me + i, n), me).start())

    kv[0, rows_of(me), :] = stage[rows_of(me // copies), :]

    @pl.when(s == 0)
    def _():
        kv[1] = jnp.zeros(kv.shape[1:], kv.dtype)

    @pl.when(s == n_seq - 1)
    def _():
        ret[1] = jnp.zeros(ret.shape[1:], ret.dtype)

    slot_col = lax.broadcasted_iota(jnp.int32, (half, cols), 1)
    used = slot_col % pad < vision
    columns = jnp.concatenate(
        [jnp.broadcast_to(mask[i:i + 1, :half].astype(jnp.float32), (HD, half)) for i in range(2)],
        axis=0,
    ).T
    keep_own, keep_prev = columns[:, :1], columns[:, HD:HD + 1]
    bias[:, :cols] = jnp.where(used & (keep_own > 0), 0.0, NEGATIVE)
    bias[:, cols:] = jnp.where(used & (keep_prev > 0), 0.0, NEGATIVE)
    live = (keep_own + keep_prev > 0).astype(jnp.float32)
    live = jnp.concatenate([live] * group, axis=0)
    own_bias = jnp.where(used[:1], 0.0, NEGATIVE)

    for load in loads:
        load.wait()
    for h in range(heads):
        at = slice(h * HD, (h + 1) * HD)
        for b in range(2):
            to = slice(h * half, (h + 1) * half)
            rows = slice(b * half, (b + 1) * half)
            qt[b, :, to] = q[rows, at].T
            dot_t[b, :, to] = do[rows, at].T

    def stacked(ref, rows, first):
        return jnp.concatenate(
            [ref[rows, (first + i) * HD:(first + i + 1) * HD] for i in range(group)], axis=0
        )

    def attend(rows, b, first, keys, values, score_bias, live_rows, grad_store):
        query = stacked(q, rows, first)
        grad = stacked(do, rows, first)
        scores = dot_nt(query, keys) + score_bias
        peak = jnp.max(scores, axis=1, keepdims=True)
        powered = jnp.exp2((scores - peak) * EXP2_SCALE)
        weights = powered * (live_rows / jnp.sum(powered, axis=1, keepdims=True))
        rounded = weights.astype(jnp.bfloat16)
        attended = dot(rounded, values)
        delta = jnp.sum(grad.astype(jnp.float32) * attended, axis=1, keepdims=True)
        grad_weights = dot_nt(grad, values)
        grad_scores = (weights * (grad_weights - delta)).astype(jnp.bfloat16)
        for i in range(group):
            at = slice((first + i) * HD, (first + i + 1) * HD)
            att[rows, at] = attended[i * half:(i + 1) * half].astype(jnp.bfloat16)
        to = slice(first * half, (first + group) * half)
        grad_store[to, :] = grad_scores
        return dot(qt[b, :, to], grad_scores), dot(dot_t[b, :, to], rounded)

    def put(b, key_sum, value_sum):
        part[b, :, :HD] = (key_sum * SCALE).T.astype(jnp.bfloat16)
        part[b, :, HD:] = value_sum.T.astype(jnp.bfloat16)

    def query_grads(rows, grad_store, keys):
        for first in firsts:
            grads = dot(grad_store[first * half:(first + group) * half, :], keys) * SCALE
            for i in range(group):
                at = slice((first + i) * HD, (first + i + 1) * HD)
                gq[rows, at] = grads[i * half:(i + 1) * half].astype(jnp.bfloat16)

    upper, lower = slice(half, tokens), slice(0, half)
    firsts = list(range(0, heads, group))
    cut = len(firsts) // 2

    each(n - 1, lambda i: kv_copy(0, s, me, lax.rem(me + 1 + i, n)).wait_recv())
    key_sum, value_sum = 0.0, 0.0
    keys, values = kv[0, :, :HD], kv[0, :, HD:]
    for first in firsts[:cut]:
        key_term, value_term = attend(upper, 1, first, keys, values, own_bias, 1.0, gs_upper)
        key_sum, value_sum = key_sum + key_term, value_sum + value_term

    @pl.when(not_first)
    def _():
        each(n, lambda i: kv_copy(1, s, me, lax.rem(me + i, n)).wait_recv())

    both_keys = kv[:, :, :HD].reshape(2 * cols, HD)
    both_values = kv[:, :, HD:].reshape(2 * cols, HD)
    both_bias = jnp.concatenate([bias[...]] * group, axis=0)
    key_both, value_both = 0.0, 0.0
    for first in firsts:
        key_term, value_term = attend(
            lower, 0, first, both_keys, both_values, both_bias, live, gs_lower
        )
        key_both, value_both = key_both + key_term, value_both + value_term
    put(1, key_both[:, cols:], value_both[:, cols:])

    @pl.when(not_first)
    def _():
        each(n, lambda i: part_copy(1, s - 1, lax.rem(me + i, n), me).start())

    key_sum, value_sum = key_sum + key_both[:, :cols], value_sum + value_both[:, :cols]
    for first in firsts[cut:]:
        key_term, value_term = attend(upper, 1, first, keys, values, own_bias, 1.0, gs_upper)
        key_sum, value_sum = key_sum + key_term, value_sum + value_term
    put(0, key_sum, value_sum)
    each(n - 1, lambda i: part_copy(0, s, lax.rem(me + 1 + i, n), me).start())
    ret[0, rows_of(me), :] = part[0, rows_of(me), :]
    query_grads(upper, gs_upper, keys)
    query_grads(lower, gs_lower, both_keys)

    gather = slot_map(pad, vision, True)
    each(n - 1, lambda i: part_copy(0, s, me, lax.rem(me + 1 + i, n)).wait_recv())

    @pl.when(not_last)
    def _():
        each(n, lambda i: part_copy(1, s, me, lax.rem(me + i, n)).wait_recv())

    total = ret[0].astype(jnp.float32) + ret[1].astype(jnp.float32)
    total = total.reshape(KVH, copies, pad, 2 * HD).sum(axis=1).reshape(KVH * pad, 2 * HD)
    grads = dot(gather, total.astype(jnp.bfloat16)).astype(jnp.bfloat16)
    gk_ref[...] = grads[:, :HD]
    gv_ref[...] = grads[:, HD:]

    each(n - 1, lambda i: kv_copy(0, s, lax.rem(me + 1 + i, n), me).wait_send())
    each(n - 1, lambda i: part_copy(0, s, lax.rem(me + 1 + i, n), me).wait_send())

    @pl.when(not_last)
    def _():
        each(n, lambda i: kv_copy(1, s + 1, lax.rem(me + i, n), me).wait_send())

    @pl.when(not_first)
    def _():
        each(n, lambda i: part_copy(1, s - 1, lax.rem(me + i, n), me).wait_send())


def copy_out(*refs):
    count = len(refs) // 2
    copies = [pltpu.make_async_copy(refs[i], refs[count + i], refs[-1].at[i]) for i in range(count)]
    for copy in copies:
        copy.start()
    for copy in copies:
        copy.wait()


def per_device(n_seq, n, queries, keys, values, cotangent, mask):
    tokens, width = queries.shape
    vision = keys.shape[1]
    pad = -(-vision // 16) * 16
    heads = width // HD
    group = min(2, heads)
    half = tokens // 2
    cols = n * pad
    bf16, f32 = jnp.bfloat16, jnp.float32
    vmem = pl.BlockSpec(memory_space=pltpu.VMEM)
    hbm = pl.BlockSpec(memory_space=pltpu.HBM)
    anywhere = pl.BlockSpec(memory_space=pl.ANY)
    dma = pltpu.SemaphoreType.DMA
    results = (
        jax.ShapeDtypeStruct((tokens, width), bf16),
        jax.ShapeDtypeStruct((tokens, width), bf16),
        jax.ShapeDtypeStruct((vision * KVH, HD), bf16),
        jax.ShapeDtypeStruct((vision * KVH, HD), bf16),
    )
    found = pl.pallas_call(
        functools.partial(kernel, n_seq, n, pad, vision, group),
        out_shape=results,
        in_specs=[hbm] * 5,
        out_specs=(vmem,) * 4,
        scratch_shapes=[
            pltpu.VMEM((tokens, width), bf16),
            pltpu.VMEM((tokens, width), bf16),
            pltpu.VMEM((vision * KVH, HD), bf16),
            pltpu.VMEM((vision * KVH, HD), bf16),
            pltpu.VMEM((2, tokens), mask.dtype),
            pltpu.VMEM((2, HD, heads * half), bf16),
            pltpu.VMEM((2, HD, heads * half), bf16),
            pltpu.VMEM((KVH * pad, 2 * HD), bf16),
            pltpu.VMEM((2, cols, 2 * HD), bf16),
            pltpu.VMEM((2, cols, 2 * HD), bf16),
            pltpu.VMEM((2, cols, 2 * HD), bf16),
            pltpu.VMEM((half, 2 * cols), f32),
            pltpu.VMEM((heads * half, 2 * cols), bf16),
            pltpu.VMEM((heads * half, cols), bf16),
            dma((2, 2)),
            dma((3,)),
            dma((2, n)),
            dma((2, n)),
            dma((2, n)),
            dma((2, n)),
        ],
        compiler_params=pltpu.CompilerParams(
            collective_id=0, has_side_effects=True, vmem_limit_bytes=VMEM_LIMIT
        ),
    )(
        queries,
        keys.reshape(vision * KVH, HD),
        values.reshape(vision * KVH, HD),
        cotangent,
        mask.T,
    )
    attended, grad_query, grad_keys, grad_values = pl.pallas_call(
        copy_out,
        out_shape=results,
        in_specs=[anywhere] * 4,
        out_specs=(hbm,) * 4,
        scratch_shapes=[dma((4,))],
    )(*found)
    shape = (1, vision, KVH, HD)
    return attended, grad_query, grad_keys.reshape(shape), grad_values.reshape(shape)


def solution(mesh):
    return jax.shard_map(
        functools.partial(per_device, mesh.shape["seq"], mesh.shape["head"]),
        mesh=mesh,
        in_specs=(
            P("seq", "head"),
            P("seq", "head", None, None),
            P("seq", "head", None, None),
            P("seq", "head"),
            P("seq", None),
        ),
        out_specs=(
            P("seq", "head"),
            P("seq", "head"),
            P("seq", "head", None, None),
            P("seq", "head", None, None),
        ),
        check_vma=False,
    )
```

```python
import functools
import math

import jax
import jax.numpy as jnp
from jax import lax
from jax.experimental import pallas as pl
from jax.experimental.pallas import tpu as pltpu
from jax.sharding import PartitionSpec as P

KVH = 8
HD = 128
NEGATIVE = -1e30
VMEM_LIMIT = 58 * 1024 * 1024
MESH = pl.DeviceIdType.MESH
SCALE = HD ** -0.5
EXP2_SCALE = SCALE * math.log2(math.e)


def dot(a, b):
    return jnp.dot(a, b, preferred_element_type=jnp.float32)


def dot_nt(a, b):
    return lax.dot_general(a, b, (((1,), (1,)), ((), ())), preferred_element_type=jnp.float32)


def each(count, body):
    if count <= 8:
        for i in range(count):
            body(i)
    else:
        lax.fori_loop(0, count, lambda i, c: (body(i), c)[1], 0)


def slot_map(pad, vision, transposed):
    shape = (vision * KVH, KVH * pad) if transposed else (KVH * pad, vision * KVH)
    slot = lax.broadcasted_iota(jnp.int32, shape, 1 if transposed else 0)
    row = lax.broadcasted_iota(jnp.int32, shape, 0 if transposed else 1)
    head, token = slot // pad, slot % pad
    return jnp.where((token < vision) & (row == token * KVH + head), 1.0, 0.0).astype(jnp.bfloat16)


def kernel(
    n_seq, n, pad, vision, group,
    q_hbm, k_hbm, v_hbm, do_hbm, mask_hbm,
    att_hbm, gq_hbm, gk_ref, gv_ref,
    q, do, att, gq, k_own, v_own, mask, qt, dot_t, stage, kv, part, ret, bias, gs_lower, gs_upper,
    in_sem, out_sem, small_sem, kv_send, kv_recv, part_send, part_recv,
):
    s = lax.axis_index("seq")
    me = lax.axis_index("head")
    copies = n // KVH
    tokens, width = q.shape
    heads = width // HD
    half = tokens // 2
    cols = n * pad
    not_first = s > 0
    not_last = s < n_seq - 1

    small = []
    for i, (src, dst) in enumerate(((k_hbm, k_own), (v_hbm, v_own), (mask_hbm, mask))):
        load = pltpu.make_async_copy(src, dst, small_sem.at[i])
        load.start()
        small.append(load)
    loads = []
    for i, rows in enumerate((pl.ds(half, half), pl.ds(0, half))):
        for k, (src, dst) in enumerate(((q_hbm, q), (do_hbm, do))):
            load = pltpu.make_async_copy(src.at[rows], dst.at[rows], in_sem.at[i, k])
            load.start()
            loads.append(load)

    barrier = pltpu.get_barrier_semaphore()

    def greet(block, peer):
        pl.semaphore_signal(
            barrier, inc=1, device_id={"seq": block, "head": peer}, device_id_type=MESH
        )

    each(n - 1, lambda i: greet(s, lax.rem(me + 1 + i, n)))

    @pl.when(not_first)
    def _():
        each(n, lambda i: greet(s - 1, lax.rem(me + i, n)))

    @pl.when(not_last)
    def _():
        each(n, lambda i: greet(s + 1, lax.rem(me + i, n)))

    for load in small:
        load.wait()
    spread = slot_map(pad, vision, False)
    stage[:, :HD] = dot(spread, k_own[...]).astype(jnp.bfloat16)
    stage[:, HD:] = dot(spread, v_own[...]).astype(jnp.bfloat16)

    def rows_of(index):
        return pl.ds(pl.multiple_of(index * pad, pad), pad)

    def kv_copy(b, block, peer, source):
        return pltpu.make_async_remote_copy(
            src_ref=stage.at[rows_of(peer // copies)],
            dst_ref=kv.at[b, rows_of(source)],
            send_sem=kv_send.at[b, peer],
            recv_sem=kv_recv.at[b, source],
            device_id={"seq": block, "head": peer},
            device_id_type=MESH,
        )

    def part_copy(b, block, peer, source):
        return pltpu.make_async_remote_copy(
            src_ref=part.at[b, rows_of(peer)],
            dst_ref=ret.at[b, rows_of(source)],
            send_sem=part_send.at[b, peer],
            recv_sem=part_recv.at[b, source],
            device_id={"seq": block, "head": peer},
            device_id_type=MESH,
        )

    pl.semaphore_wait(
        barrier, (n - 1) + n * not_first.astype(jnp.int32) + n * not_last.astype(jnp.int32)
    )

    each(n - 1, lambda i: kv_copy(0, s, lax.rem(me + 1 + i, n), me).start())

    @pl.when(not_last)
    def _():
        each(n, lambda i: kv_copy(1, s + 1, lax.rem(me + i, n), me).start())

    kv[0, rows_of(me), :] = stage[rows_of(me // copies), :]

    @pl.when(s == 0)
    def _():
        kv[1] = jnp.zeros(kv.shape[1:], kv.dtype)

    @pl.when(s == n_seq - 1)
    def _():
        ret[1] = jnp.zeros(ret.shape[1:], ret.dtype)

    slot_col = lax.broadcasted_iota(jnp.int32, (half, cols), 1)
    used = slot_col % pad < vision
    columns = jnp.concatenate(
        [jnp.broadcast_to(mask[i:i + 1, :half].astype(jnp.float32), (HD, half)) for i in range(2)],
        axis=0,
    ).T
    keep_own, keep_prev = columns[:, :1], columns[:, HD:HD + 1]
    bias[:, :cols] = jnp.where(used & (keep_own > 0), 0.0, NEGATIVE)
    bias[:, cols:] = jnp.where(used & (keep_prev > 0), 0.0, NEGATIVE)
    live = (keep_own + keep_prev > 0).astype(jnp.float32)
    live = jnp.concatenate([live] * group, axis=0)
    own_bias = jnp.where(used[:1], 0.0, NEGATIVE)

    for load in loads:
        load.wait()
    for h in range(heads):
        at = slice(h * HD, (h + 1) * HD)
        for b in range(2):
            to = slice(h * half, (h + 1) * half)
            rows = slice(b * half, (b + 1) * half)
            qt[b, :, to] = q[rows, at].T
            dot_t[b, :, to] = do[rows, at].T

    def stacked(ref, rows, first):
        return jnp.concatenate(
            [ref[rows, (first + i) * HD:(first + i + 1) * HD] for i in range(group)], axis=0
        )

    def attend(rows, b, first, keys, values, score_bias, live_rows, grad_store):
        query = stacked(q, rows, first)
        grad = stacked(do, rows, first)
        scores = dot_nt(query, keys) + score_bias
        peak = jnp.max(scores, axis=1, keepdims=True)
        powered = jnp.exp2((scores - peak) * EXP2_SCALE)
        weights = powered * (live_rows / jnp.sum(powered, axis=1, keepdims=True))
        rounded = weights.astype(jnp.bfloat16)
        attended = dot(rounded, values)
        delta = jnp.sum(grad.astype(jnp.float32) * attended, axis=1, keepdims=True)
        grad_weights = dot_nt(grad, values)
        grad_scores = (weights * (grad_weights - delta)).astype(jnp.bfloat16)
        for i in range(group):
            at = slice((first + i) * HD, (first + i + 1) * HD)
            att[rows, at] = attended[i * half:(i + 1) * half].astype(jnp.bfloat16)
        to = slice(first * half, (first + group) * half)
        grad_store[to, :] = grad_scores
        return dot(qt[b, :, to], grad_scores), dot(dot_t[b, :, to], rounded)

    def put(b, key_sum, value_sum):
        part[b, :, :HD] = (key_sum * SCALE).T.astype(jnp.bfloat16)
        part[b, :, HD:] = value_sum.T.astype(jnp.bfloat16)

    def query_grads(rows, grad_store, keys):
        for first in firsts:
            grads = dot(grad_store[first * half:(first + group) * half, :], keys) * SCALE
            for i in range(group):
                at = slice((first + i) * HD, (first + i + 1) * HD)
                gq[rows, at] = grads[i * half:(i + 1) * half].astype(jnp.bfloat16)

    stores = []

    def write_out(src, dst, b, k):
        rows = pl.ds(b * half, half)
        store = pltpu.make_async_copy(src.at[rows], dst.at[rows], out_sem.at[b, k])
        store.start()
        stores.append(store)

    upper, lower = slice(half, tokens), slice(0, half)
    firsts = list(range(0, heads, group))
    cut = len(firsts) // 2

    each(n - 1, lambda i: kv_copy(0, s, me, lax.rem(me + 1 + i, n)).wait_recv())
    key_sum, value_sum = 0.0, 0.0
    keys, values = kv[0, :, :HD], kv[0, :, HD:]
    for first in firsts[:cut]:
        key_term, value_term = attend(upper, 1, first, keys, values, own_bias, 1.0, gs_upper)
        key_sum, value_sum = key_sum + key_term, value_sum + value_term

    @pl.when(not_first)
    def _():
        each(n, lambda i: kv_copy(1, s, me, lax.rem(me + i, n)).wait_recv())

    both_keys = kv[:, :, :HD].reshape(2 * cols, HD)
    both_values = kv[:, :, HD:].reshape(2 * cols, HD)
    both_bias = jnp.concatenate([bias[...]] * group, axis=0)
    key_both, value_both = 0.0, 0.0
    for first in firsts:
        key_term, value_term = attend(
            lower, 0, first, both_keys, both_values, both_bias, live, gs_lower
        )
        key_both, value_both = key_both + key_term, value_both + value_term
    put(1, key_both[:, cols:], value_both[:, cols:])

    @pl.when(not_first)
    def _():
        each(n, lambda i: part_copy(1, s - 1, lax.rem(me + i, n), me).start())

    write_out(att, att_hbm, 0, 0)
    key_sum, value_sum = key_sum + key_both[:, :cols], value_sum + value_both[:, :cols]
    for first in firsts[cut:]:
        key_term, value_term = attend(upper, 1, first, keys, values, own_bias, 1.0, gs_upper)
        key_sum, value_sum = key_sum + key_term, value_sum + value_term
    put(0, key_sum, value_sum)
    each(n - 1, lambda i: part_copy(0, s, lax.rem(me + 1 + i, n), me).start())
    ret[0, rows_of(me), :] = part[0, rows_of(me), :]
    write_out(att, att_hbm, 1, 0)
    query_grads(upper, gs_upper, keys)
    write_out(gq, gq_hbm, 1, 1)
    query_grads(lower, gs_lower, both_keys)
    write_out(gq, gq_hbm, 0, 1)

    gather = slot_map(pad, vision, True)
    each(n - 1, lambda i: part_copy(0, s, me, lax.rem(me + 1 + i, n)).wait_recv())

    @pl.when(not_last)
    def _():
        each(n, lambda i: part_copy(1, s, me, lax.rem(me + i, n)).wait_recv())

    total = ret[0].astype(jnp.float32) + ret[1].astype(jnp.float32)
    total = total.reshape(KVH, copies, pad, 2 * HD).sum(axis=1).reshape(KVH * pad, 2 * HD)
    grads = dot(gather, total.astype(jnp.bfloat16)).astype(jnp.bfloat16)
    gk_ref[...] = grads[:, :HD]
    gv_ref[...] = grads[:, HD:]

    each(n - 1, lambda i: kv_copy(0, s, lax.rem(me + 1 + i, n), me).wait_send())
    each(n - 1, lambda i: part_copy(0, s, lax.rem(me + 1 + i, n), me).wait_send())

    @pl.when(not_last)
    def _():
        each(n, lambda i: kv_copy(1, s + 1, lax.rem(me + i, n), me).wait_send())

    @pl.when(not_first)
    def _():
        each(n, lambda i: part_copy(1, s - 1, lax.rem(me + i, n), me).wait_send())

    for store in stores:
        store.wait()


def copy_out(*refs):
    count = (len(refs) - 2) // 3
    sources, targets, held = refs[:count], refs[count:2 * count], refs[2 * count:3 * count]
    load_sem, store_sem = refs[3 * count:]
    loads = [pltpu.make_async_copy(a, b, load_sem.at[i]) for i, (a, b) in enumerate(zip(sources, held))]
    stores = [pltpu.make_async_copy(a, b, store_sem.at[i]) for i, (a, b) in enumerate(zip(held, targets))]
    for load in loads:
        load.start()
    for load, store in zip(loads, stores):
        load.wait()
        store.start()
    for store in stores:
        store.wait()


def per_device(n_seq, n, queries, keys, values, cotangent, mask):
    tokens, width = queries.shape
    vision = keys.shape[1]
    pad = -(-vision // 16) * 16
    heads = width // HD
    group = min(4, heads)
    half = tokens // 2
    cols = n * pad
    bf16, f32 = jnp.bfloat16, jnp.float32
    vmem = pl.BlockSpec(memory_space=pltpu.VMEM)
    hbm = pl.BlockSpec(memory_space=pltpu.HBM)
    dma = pltpu.SemaphoreType.DMA
    results = (
        jax.ShapeDtypeStruct((tokens, width), bf16),
        jax.ShapeDtypeStruct((tokens, width), bf16),
        jax.ShapeDtypeStruct((vision * KVH, HD), bf16),
        jax.ShapeDtypeStruct((vision * KVH, HD), bf16),
    )
    found = pl.pallas_call(
        functools.partial(kernel, n_seq, n, pad, vision, group),
        out_shape=results,
        in_specs=[hbm] * 5,
        out_specs=(hbm, hbm, vmem, vmem),
        scratch_shapes=[
            pltpu.VMEM((tokens, width), bf16),
            pltpu.VMEM((tokens, width), bf16),
            pltpu.VMEM((tokens, width), bf16),
            pltpu.VMEM((tokens, width), bf16),
            pltpu.VMEM((vision * KVH, HD), bf16),
            pltpu.VMEM((vision * KVH, HD), bf16),
            pltpu.VMEM((2, tokens), mask.dtype),
            pltpu.VMEM((2, HD, heads * half), bf16),
            pltpu.VMEM((2, HD, heads * half), bf16),
            pltpu.VMEM((KVH * pad, 2 * HD), bf16),
            pltpu.VMEM((2, cols, 2 * HD), bf16),
            pltpu.VMEM((2, cols, 2 * HD), bf16),
            pltpu.VMEM((2, cols, 2 * HD), bf16),
            pltpu.VMEM((half, 2 * cols), f32),
            pltpu.VMEM((heads * half, 2 * cols), bf16),
            pltpu.VMEM((heads * half, cols), bf16),
            dma((2, 2)),
            dma((2, 2)),
            dma((3,)),
            dma((2, n)),
            dma((2, n)),
            dma((2, n)),
            dma((2, n)),
        ],
        compiler_params=pltpu.CompilerParams(
            collective_id=0, has_side_effects=True, vmem_limit_bytes=VMEM_LIMIT
        ),
    )(
        queries,
        keys.reshape(vision * KVH, HD),
        values.reshape(vision * KVH, HD),
        cotangent,
        mask.T,
    )
    attended, grad_query, grad_keys, grad_values = pl.pallas_call(
        copy_out,
        out_shape=results,
        in_specs=[hbm] * 4,
        out_specs=(hbm,) * 4,
        scratch_shapes=[pltpu.VMEM(r.shape, bf16) for r in results] + [dma((4,)), dma((4,))],
        compiler_params=pltpu.CompilerParams(vmem_limit_bytes=VMEM_LIMIT),
    )(*found)
    shape = (1, vision, KVH, HD)
    return attended, grad_query, grad_keys.reshape(shape), grad_values.reshape(shape)


def solution(mesh):
    return jax.shard_map(
        functools.partial(per_device, mesh.shape["seq"], mesh.shape["head"]),
        mesh=mesh,
        in_specs=(
            P("seq", "head"),
            P("seq", "head", None, None),
            P("seq", "head", None, None),
            P("seq", "head"),
            P("seq", None),
        ),
        out_specs=(
            P("seq", "head"),
            P("seq", "head"),
            P("seq", "head", None, None),
            P("seq", "head", None, None),
        ),
        check_vma=False,
    )
```

```python
import functools
import math

import jax
import jax.numpy as jnp
from jax import lax
from jax.experimental import pallas as pl
from jax.experimental.pallas import tpu as pltpu
from jax.sharding import PartitionSpec as P

KVH = 8
HD = 128
NEGATIVE = -1e30
VMEM_LIMIT = 58 * 1024 * 1024
MESH = pl.DeviceIdType.MESH
SCALE = HD ** -0.5
EXP2_SCALE = SCALE * math.log2(math.e)


def dot(a, b):
    return jnp.dot(a, b, preferred_element_type=jnp.float32)


def dot_nt(a, b):
    return lax.dot_general(a, b, (((1,), (1,)), ((), ())), preferred_element_type=jnp.float32)


def each(count, body):
    if count <= 8:
        for i in range(count):
            body(i)
    else:
        lax.fori_loop(0, count, lambda i, c: (body(i), c)[1], 0)


def slot_map(pad, vision, transposed):
    shape = (vision * KVH, KVH * pad) if transposed else (KVH * pad, vision * KVH)
    slot = lax.broadcasted_iota(jnp.int32, shape, 1 if transposed else 0)
    row = lax.broadcasted_iota(jnp.int32, shape, 0 if transposed else 1)
    head, token = slot // pad, slot % pad
    return jnp.where((token < vision) & (row == token * KVH + head), 1.0, 0.0).astype(jnp.bfloat16)


def kernel(
    n_seq, n, pad, vision, group,
    q_hbm, k_hbm, v_hbm, do_hbm, mask_hbm,
    att_hbm, gq_hbm, gk_ref, gv_ref,
    q, do, att, gq, k_own, v_own, mask, qt, dot_t, stage, kv, part, ret, bias, gs_lower, gs_upper,
    in_sem, out_sem, small_sem, kv_send, kv_recv, part_send, part_recv,
):
    s = lax.axis_index("seq")
    me = lax.axis_index("head")
    copies = n // KVH
    tokens, width = q.shape
    heads = width // HD
    half = tokens // 2
    cols = n * pad
    not_first = s > 0
    not_last = s < n_seq - 1

    small = []
    for i, (src, dst) in enumerate(((k_hbm, k_own), (v_hbm, v_own), (mask_hbm, mask))):
        load = pltpu.make_async_copy(src, dst, small_sem.at[i])
        load.start()
        small.append(load)
    loads = []
    for i, rows in enumerate((pl.ds(half, half), pl.ds(0, half))):
        for k, (src, dst) in enumerate(((q_hbm, q), (do_hbm, do))):
            load = pltpu.make_async_copy(src.at[rows], dst.at[rows], in_sem.at[i, k])
            load.start()
            loads.append(load)

    barrier = pltpu.get_barrier_semaphore()

    def greet(block, peer):
        pl.semaphore_signal(
            barrier, inc=1, device_id={"seq": block, "head": peer}, device_id_type=MESH
        )

    each(n - 1, lambda i: greet(s, lax.rem(me + 1 + i, n)))

    @pl.when(not_first)
    def _():
        each(n, lambda i: greet(s - 1, lax.rem(me + i, n)))

    @pl.when(not_last)
    def _():
        each(n, lambda i: greet(s + 1, lax.rem(me + i, n)))

    for load in small:
        load.wait()
    spread = slot_map(pad, vision, False)
    stage[:, :HD] = dot(spread, k_own[...]).astype(jnp.bfloat16)
    stage[:, HD:] = dot(spread, v_own[...]).astype(jnp.bfloat16)

    def rows_of(index):
        return pl.ds(pl.multiple_of(index * pad, pad), pad)

    def kv_copy(b, block, peer, source):
        return pltpu.make_async_remote_copy(
            src_ref=stage.at[rows_of(peer // copies)],
            dst_ref=kv.at[b, rows_of(source)],
            send_sem=kv_send.at[b, peer],
            recv_sem=kv_recv.at[b, source],
            device_id={"seq": block, "head": peer},
            device_id_type=MESH,
        )

    def part_copy(b, block, peer, source):
        return pltpu.make_async_remote_copy(
            src_ref=part.at[b, rows_of(peer)],
            dst_ref=ret.at[b, rows_of(source)],
            send_sem=part_send.at[b, peer],
            recv_sem=part_recv.at[b, source],
            device_id={"seq": block, "head": peer},
            device_id_type=MESH,
        )

    pl.semaphore_wait(
        barrier, (n - 1) + n * not_first.astype(jnp.int32) + n * not_last.astype(jnp.int32)
    )

    each(n - 1, lambda i: kv_copy(0, s, lax.rem(me + 1 + i, n), me).start())

    @pl.when(not_last)
    def _():
        each(n, lambda i: kv_copy(1, s + 1, lax.rem(me + i, n), me).start())

    kv[0, rows_of(me), :] = stage[rows_of(me // copies), :]

    @pl.when(s == 0)
    def _():
        kv[1] = jnp.zeros(kv.shape[1:], kv.dtype)

    @pl.when(s == n_seq - 1)
    def _():
        ret[1] = jnp.zeros(ret.shape[1:], ret.dtype)

    slot_col = lax.broadcasted_iota(jnp.int32, (half, cols), 1)
    used = slot_col % pad < vision
    columns = jnp.concatenate(
        [jnp.broadcast_to(mask[i:i + 1, :half].astype(jnp.float32), (HD, half)) for i in range(2)],
        axis=0,
    ).T
    keep_own, keep_prev = columns[:, :1], columns[:, HD:HD + 1]
    bias[:, :cols] = jnp.where(used & (keep_own > 0), 0.0, NEGATIVE)
    bias[:, cols:] = jnp.where(used & (keep_prev > 0), 0.0, NEGATIVE)
    live = (keep_own + keep_prev > 0).astype(jnp.float32)
    live = jnp.concatenate([live] * group, axis=0)
    own_bias = jnp.where(used[:1], 0.0, NEGATIVE)

    for load in loads:
        load.wait()
    for h in range(heads):
        at = slice(h * HD, (h + 1) * HD)
        for b in range(2):
            to = slice(h * half, (h + 1) * half)
            rows = slice(b * half, (b + 1) * half)
            qt[b, :, to] = q[rows, at].T
            dot_t[b, :, to] = do[rows, at].T

    def stacked(ref, rows, first):
        return jnp.concatenate(
            [ref[rows, (first + i) * HD:(first + i + 1) * HD] for i in range(group)], axis=0
        )

    def attend(rows, b, first, keys, values, score_bias, live_rows, grad_store):
        query = stacked(q, rows, first)
        grad = stacked(do, rows, first)
        scores = dot_nt(query, keys) + score_bias
        peak = jnp.max(scores, axis=1, keepdims=True)
        powered = jnp.exp2((scores - peak) * EXP2_SCALE)
        weights = powered * (live_rows / jnp.sum(powered, axis=1, keepdims=True))
        rounded = weights.astype(jnp.bfloat16)
        attended = dot(rounded, values)
        delta = jnp.sum(grad.astype(jnp.float32) * attended, axis=1, keepdims=True)
        grad_weights = dot_nt(grad, values)
        grad_scores = (weights * (grad_weights - delta)).astype(jnp.bfloat16)
        for i in range(group):
            at = slice((first + i) * HD, (first + i + 1) * HD)
            att[rows, at] = attended[i * half:(i + 1) * half].astype(jnp.bfloat16)
        to = slice(first * half, (first + group) * half)
        grad_store[to, :] = grad_scores
        return dot(qt[b, :, to], grad_scores), dot(dot_t[b, :, to], rounded)

    def put(b, key_sum, value_sum):
        part[b, :, :HD] = (key_sum * SCALE).T.astype(jnp.bfloat16)
        part[b, :, HD:] = value_sum.T.astype(jnp.bfloat16)

    def query_grads(rows, grad_store, keys):
        for first in firsts:
            grads = dot(grad_store[first * half:(first + group) * half, :], keys) * SCALE
            for i in range(group):
                at = slice((first + i) * HD, (first + i + 1) * HD)
                gq[rows, at] = grads[i * half:(i + 1) * half].astype(jnp.bfloat16)

    stores = []

    def write_out(src, dst, b, k):
        rows = pl.ds(b * half, half)
        store = pltpu.make_async_copy(src.at[rows], dst.at[rows], out_sem.at[b, k])
        store.start()
        stores.append(store)

    upper, lower = slice(half, tokens), slice(0, half)
    firsts = list(range(0, heads, group))
    cut = len(firsts) // 2

    each(n - 1, lambda i: kv_copy(0, s, me, lax.rem(me + 1 + i, n)).wait_recv())
    key_sum, value_sum = 0.0, 0.0
    keys, values = kv[0, :, :HD], kv[0, :, HD:]
    for first in firsts[:cut]:
        key_term, value_term = attend(upper, 1, first, keys, values, own_bias, 1.0, gs_upper)
        key_sum, value_sum = key_sum + key_term, value_sum + value_term

    @pl.when(not_first)
    def _():
        each(n, lambda i: kv_copy(1, s, me, lax.rem(me + i, n)).wait_recv())

    both_keys = kv[:, :, :HD].reshape(2 * cols, HD)
    both_values = kv[:, :, HD:].reshape(2 * cols, HD)
    both_bias = jnp.concatenate([bias[...]] * group, axis=0)
    key_both, value_both = 0.0, 0.0
    for first in firsts:
        key_term, value_term = attend(
            lower, 0, first, both_keys, both_values, both_bias, live, gs_lower
        )
        key_both, value_both = key_both + key_term, value_both + value_term
    put(1, key_both[:, cols:], value_both[:, cols:])

    @pl.when(not_first)
    def _():
        each(n, lambda i: part_copy(1, s - 1, lax.rem(me + i, n), me).start())

    write_out(att, att_hbm, 0, 0)
    key_sum, value_sum = key_sum + key_both[:, :cols], value_sum + value_both[:, :cols]
    for first in firsts[cut:]:
        key_term, value_term = attend(upper, 1, first, keys, values, own_bias, 1.0, gs_upper)
        key_sum, value_sum = key_sum + key_term, value_sum + value_term
    put(0, key_sum, value_sum)
    each(n - 1, lambda i: part_copy(0, s, lax.rem(me + 1 + i, n), me).start())
    ret[0, rows_of(me), :] = part[0, rows_of(me), :]
    write_out(att, att_hbm, 1, 0)
    query_grads(upper, gs_upper, keys)
    write_out(gq, gq_hbm, 1, 1)
    query_grads(lower, gs_lower, both_keys)
    write_out(gq, gq_hbm, 0, 1)

    gather = slot_map(pad, vision, True)
    each(n - 1, lambda i: part_copy(0, s, me, lax.rem(me + 1 + i, n)).wait_recv())

    @pl.when(not_last)
    def _():
        each(n, lambda i: part_copy(1, s, me, lax.rem(me + i, n)).wait_recv())

    total = ret[0].astype(jnp.float32) + ret[1].astype(jnp.float32)
    total = total.reshape(KVH, copies, pad, 2 * HD).sum(axis=1).reshape(KVH * pad, 2 * HD)
    grads = dot(gather, total.astype(jnp.bfloat16)).astype(jnp.bfloat16)
    gk_ref[...] = grads[:, :HD]
    gv_ref[...] = grads[:, HD:]

    each(n - 1, lambda i: kv_copy(0, s, lax.rem(me + 1 + i, n), me).wait_send())
    each(n - 1, lambda i: part_copy(0, s, lax.rem(me + 1 + i, n), me).wait_send())

    @pl.when(not_last)
    def _():
        each(n, lambda i: kv_copy(1, s + 1, lax.rem(me + i, n), me).wait_send())

    @pl.when(not_first)
    def _():
        each(n, lambda i: part_copy(1, s - 1, lax.rem(me + i, n), me).wait_send())

    for store in stores:
        store.wait()


def copy_out(*refs):
    count = (len(refs) - 2) // 3
    sources, targets, held = refs[:count], refs[count:2 * count], refs[2 * count:3 * count]
    load_sem, store_sem = refs[3 * count:]
    loads = [pltpu.make_async_copy(a, b, load_sem.at[i]) for i, (a, b) in enumerate(zip(sources, held))]
    stores = [pltpu.make_async_copy(a, b, store_sem.at[i]) for i, (a, b) in enumerate(zip(held, targets))]
    for load in loads:
        load.start()
    for load, store in zip(loads, stores):
        load.wait()
        store.start()
    for store in stores:
        store.wait()


def per_device(n_seq, n, queries, keys, values, cotangent, mask):
    tokens, width = queries.shape
    vision = keys.shape[1]
    pad = -(-vision // 16) * 16
    heads = width // HD
    group = min(8, heads)
    half = tokens // 2
    cols = n * pad
    bf16, f32 = jnp.bfloat16, jnp.float32
    vmem = pl.BlockSpec(memory_space=pltpu.VMEM)
    hbm = pl.BlockSpec(memory_space=pltpu.HBM)
    dma = pltpu.SemaphoreType.DMA
    results = (
        jax.ShapeDtypeStruct((tokens, width), bf16),
        jax.ShapeDtypeStruct((tokens, width), bf16),
        jax.ShapeDtypeStruct((vision * KVH, HD), bf16),
        jax.ShapeDtypeStruct((vision * KVH, HD), bf16),
    )
    found = pl.pallas_call(
        functools.partial(kernel, n_seq, n, pad, vision, group),
        out_shape=results,
        in_specs=[hbm] * 5,
        out_specs=(hbm, hbm, vmem, vmem),
        scratch_shapes=[
            pltpu.VMEM((tokens, width), bf16),
            pltpu.VMEM((tokens, width), bf16),
            pltpu.VMEM((tokens, width), bf16),
            pltpu.VMEM((tokens, width), bf16),
            pltpu.VMEM((vision * KVH, HD), bf16),
            pltpu.VMEM((vision * KVH, HD), bf16),
            pltpu.VMEM((2, tokens), mask.dtype),
            pltpu.VMEM((2, HD, heads * half), bf16),
            pltpu.VMEM((2, HD, heads * half), bf16),
            pltpu.VMEM((KVH * pad, 2 * HD), bf16),
            pltpu.VMEM((2, cols, 2 * HD), bf16),
            pltpu.VMEM((2, cols, 2 * HD), bf16),
            pltpu.VMEM((2, cols, 2 * HD), bf16),
            pltpu.VMEM((half, 2 * cols), f32),
            pltpu.VMEM((heads * half, 2 * cols), bf16),
            pltpu.VMEM((heads * half, cols), bf16),
            dma((2, 2)),
            dma((2, 2)),
            dma((3,)),
            dma((2, n)),
            dma((2, n)),
            dma((2, n)),
            dma((2, n)),
        ],
        compiler_params=pltpu.CompilerParams(
            collective_id=0, has_side_effects=True, vmem_limit_bytes=VMEM_LIMIT
        ),
    )(
        queries,
        keys.reshape(vision * KVH, HD),
        values.reshape(vision * KVH, HD),
        cotangent,
        mask.T,
    )
    attended, grad_query, grad_keys, grad_values = pl.pallas_call(
        copy_out,
        out_shape=results,
        in_specs=[hbm] * 4,
        out_specs=(hbm,) * 4,
        scratch_shapes=[pltpu.VMEM(r.shape, bf16) for r in results] + [dma((4,)), dma((4,))],
        compiler_params=pltpu.CompilerParams(vmem_limit_bytes=VMEM_LIMIT),
    )(*found)
    shape = (1, vision, KVH, HD)
    return attended, grad_query, grad_keys.reshape(shape), grad_values.reshape(shape)


def solution(mesh):
    return jax.shard_map(
        functools.partial(per_device, mesh.shape["seq"], mesh.shape["head"]),
        mesh=mesh,
        in_specs=(
            P("seq", "head"),
            P("seq", "head", None, None),
            P("seq", "head", None, None),
            P("seq", "head"),
            P("seq", None),
        ),
        out_specs=(
            P("seq", "head"),
            P("seq", "head"),
            P("seq", "head", None, None),
            P("seq", "head", None, None),
        ),
        check_vma=False,
    )
```

```python
import functools
import math

import jax
import jax.numpy as jnp
from jax import lax
from jax.experimental import pallas as pl
from jax.experimental.pallas import tpu as pltpu
from jax.sharding import PartitionSpec as P

KVH = 8
HD = 128
NEGATIVE = -1e30
VMEM_LIMIT = 58 * 1024 * 1024
MESH = pl.DeviceIdType.MESH
SCALE = HD ** -0.5
EXP2_SCALE = SCALE * math.log2(math.e)


def dot(a, b):
    return jnp.dot(a, b, preferred_element_type=jnp.float32)


def dot_nt(a, b):
    return lax.dot_general(a, b, (((1,), (1,)), ((), ())), preferred_element_type=jnp.float32)


def each(count, body):
    if count <= 8:
        for i in range(count):
            body(i)
    else:
        lax.fori_loop(0, count, lambda i, c: (body(i), c)[1], 0)


def slot_map(pad, vision, transposed):
    shape = (vision * KVH, KVH * pad) if transposed else (KVH * pad, vision * KVH)
    slot = lax.broadcasted_iota(jnp.int32, shape, 1 if transposed else 0)
    row = lax.broadcasted_iota(jnp.int32, shape, 0 if transposed else 1)
    head, token = slot // pad, slot % pad
    return jnp.where((token < vision) & (row == token * KVH + head), 1.0, 0.0).astype(jnp.bfloat16)


def kernel(
    n_seq, n, pad, vision, group,
    q_hbm, k_hbm, v_hbm, do_hbm, mask_hbm,
    att_hbm, gq_hbm, gk_ref, gv_ref,
    q, do, att, gq, k_own, v_own, mask, qt, dot_t, stage, kv, part, ret, bias, w_lower, w_upper, gs_lower, gs_upper,
    in_sem, out_sem, small_sem, kv_send, kv_recv, part_send, part_recv,
):
    s = lax.axis_index("seq")
    me = lax.axis_index("head")
    copies = n // KVH
    tokens, width = q.shape
    heads = width // HD
    half = tokens // 2
    cols = n * pad
    not_first = s > 0
    not_last = s < n_seq - 1

    small = []
    for i, (src, dst) in enumerate(((k_hbm, k_own), (v_hbm, v_own), (mask_hbm, mask))):
        load = pltpu.make_async_copy(src, dst, small_sem.at[i])
        load.start()
        small.append(load)
    loads = []
    for i, rows in enumerate((pl.ds(half, half), pl.ds(0, half))):
        for k, (src, dst) in enumerate(((q_hbm, q), (do_hbm, do))):
            load = pltpu.make_async_copy(src.at[rows], dst.at[rows], in_sem.at[i, k])
            load.start()
            loads.append(load)

    barrier = pltpu.get_barrier_semaphore()

    def greet(block, peer):
        pl.semaphore_signal(
            barrier, inc=1, device_id={"seq": block, "head": peer}, device_id_type=MESH
        )

    each(n - 1, lambda i: greet(s, lax.rem(me + 1 + i, n)))

    @pl.when(not_first)
    def _():
        each(n, lambda i: greet(s - 1, lax.rem(me + i, n)))

    @pl.when(not_last)
    def _():
        each(n, lambda i: greet(s + 1, lax.rem(me + i, n)))

    for load in small:
        load.wait()
    spread = slot_map(pad, vision, False)
    stage[:, :HD] = dot(spread, k_own[...]).astype(jnp.bfloat16)
    stage[:, HD:] = dot(spread, v_own[...]).astype(jnp.bfloat16)

    def rows_of(index):
        return pl.ds(pl.multiple_of(index * pad, pad), pad)

    def kv_copy(b, block, peer, source):
        return pltpu.make_async_remote_copy(
            src_ref=stage.at[rows_of(peer // copies)],
            dst_ref=kv.at[b, rows_of(source)],
            send_sem=kv_send.at[b, peer],
            recv_sem=kv_recv.at[b, source],
            device_id={"seq": block, "head": peer},
            device_id_type=MESH,
        )

    def part_copy(b, block, peer, source):
        return pltpu.make_async_remote_copy(
            src_ref=part.at[b, rows_of(peer)],
            dst_ref=ret.at[b, rows_of(source)],
            send_sem=part_send.at[b, peer],
            recv_sem=part_recv.at[b, source],
            device_id={"seq": block, "head": peer},
            device_id_type=MESH,
        )

    pl.semaphore_wait(
        barrier, (n - 1) + n * not_first.astype(jnp.int32) + n * not_last.astype(jnp.int32)
    )

    each(n - 1, lambda i: kv_copy(0, s, lax.rem(me + 1 + i, n), me).start())

    @pl.when(not_last)
    def _():
        each(n, lambda i: kv_copy(1, s + 1, lax.rem(me + i, n), me).start())

    kv[0, rows_of(me), :] = stage[rows_of(me // copies), :]

    @pl.when(s == 0)
    def _():
        kv[1] = jnp.zeros(kv.shape[1:], kv.dtype)

    @pl.when(s == n_seq - 1)
    def _():
        ret[1] = jnp.zeros(ret.shape[1:], ret.dtype)

    slot_col = lax.broadcasted_iota(jnp.int32, (half, cols), 1)
    used = slot_col % pad < vision
    columns = jnp.concatenate(
        [jnp.broadcast_to(mask[i:i + 1, :half].astype(jnp.float32), (HD, half)) for i in range(2)],
        axis=0,
    ).T
    keep_own, keep_prev = columns[:, :1], columns[:, HD:HD + 1]
    bias[:, :cols] = jnp.where(used & (keep_own > 0), 0.0, NEGATIVE)
    bias[:, cols:] = jnp.where(used & (keep_prev > 0), 0.0, NEGATIVE)
    live = (keep_own + keep_prev > 0).astype(jnp.float32)
    live = jnp.concatenate([live] * group, axis=0)
    own_bias = jnp.where(used[:1], 0.0, NEGATIVE)

    for load in loads:
        load.wait()
    for h in range(heads):
        at = slice(h * HD, (h + 1) * HD)
        for b in range(2):
            to = slice(h * half, (h + 1) * half)
            rows = slice(b * half, (b + 1) * half)
            qt[b, :, to] = q[rows, at].T
            dot_t[b, :, to] = do[rows, at].T

    def stacked(ref, rows, first):
        return jnp.concatenate(
            [ref[rows, (first + i) * HD:(first + i + 1) * HD] for i in range(group)], axis=0
        )

    ones = jnp.ones((HD, HD), jnp.bfloat16)

    def attend(rows, first, keys, values, score_bias, live_rows, weight_store, grad_store):
        query = stacked(q, rows, first)
        grad = stacked(do, rows, first)
        tiles = keys.shape[0] // HD
        scores = dot_nt(query, keys) + score_bias
        peak = jnp.max(scores, axis=1, keepdims=True)
        powered = jnp.exp2((scores - peak) * EXP2_SCALE)
        beside = jnp.concatenate([values, jnp.ones(values.shape, jnp.bfloat16)], axis=1)
        sums = dot(powered.astype(jnp.bfloat16), beside)
        ratio = live_rows / sums[:, HD:]
        attended = sums[:, :HD] * ratio
        delta = dot((grad.astype(jnp.float32) * attended).astype(jnp.bfloat16), ones)
        weights = powered * jnp.concatenate([ratio] * tiles, axis=1)
        grad_weights = dot_nt(grad, values)
        grad_scores = weights * (grad_weights - jnp.concatenate([delta] * tiles, axis=1))
        for i in range(group):
            at = slice((first + i) * HD, (first + i + 1) * HD)
            att[rows, at] = attended[i * half:(i + 1) * half].astype(jnp.bfloat16)
        to = slice(first * half, (first + group) * half)
        weight_store[to, :] = weights.astype(jnp.bfloat16)
        grad_store[to, :] = grad_scores.astype(jnp.bfloat16)

    def put(b, key_sum, value_sum):
        part[b, :, :HD] = (key_sum * SCALE).T.astype(jnp.bfloat16)
        part[b, :, HD:] = value_sum.T.astype(jnp.bfloat16)

    def query_grads(rows, grad_store, keys):
        for first in firsts:
            grads = dot(grad_store[first * half:(first + group) * half, :], keys) * SCALE
            for i in range(group):
                at = slice((first + i) * HD, (first + i + 1) * HD)
                gq[rows, at] = grads[i * half:(i + 1) * half].astype(jnp.bfloat16)

    stores = []

    def write_out(src, dst, b, k):
        rows = pl.ds(b * half, half)
        store = pltpu.make_async_copy(src.at[rows], dst.at[rows], out_sem.at[b, k])
        store.start()
        stores.append(store)

    upper, lower = slice(half, tokens), slice(0, half)
    firsts = list(range(0, heads, group))

    each(n - 1, lambda i: kv_copy(0, s, me, lax.rem(me + 1 + i, n)).wait_recv())

    @pl.when(not_first)
    def _():
        each(n, lambda i: kv_copy(1, s, me, lax.rem(me + i, n)).wait_recv())

    both_keys = kv[:, :, :HD].reshape(2 * cols, HD)
    both_values = kv[:, :, HD:].reshape(2 * cols, HD)
    both_bias = jnp.concatenate([bias[...]] * group, axis=0)
    for first in firsts:
        attend(lower, first, both_keys, both_values, both_bias, live, w_lower, gs_lower)
    put(1, dot(qt[0], gs_lower[:, cols:]), dot(dot_t[0], w_lower[:, cols:]))

    @pl.when(not_first)
    def _():
        each(n, lambda i: part_copy(1, s - 1, lax.rem(me + i, n), me).start())

    write_out(att, att_hbm, 0, 0)
    keys, values = kv[0, :, :HD], kv[0, :, HD:]
    for first in firsts:
        attend(upper, first, keys, values, own_bias, 1.0, w_upper, gs_upper)
    put(
        0,
        dot(qt[0], gs_lower[:, :cols]) + dot(qt[1], gs_upper[...]),
        dot(dot_t[0], w_lower[:, :cols]) + dot(dot_t[1], w_upper[...]),
    )
    each(n - 1, lambda i: part_copy(0, s, lax.rem(me + 1 + i, n), me).start())
    ret[0, rows_of(me), :] = part[0, rows_of(me), :]
    write_out(att, att_hbm, 1, 0)
    query_grads(upper, gs_upper, keys)
    write_out(gq, gq_hbm, 1, 1)
    query_grads(lower, gs_lower, both_keys)
    write_out(gq, gq_hbm, 0, 1)

    gather = slot_map(pad, vision, True)
    each(n - 1, lambda i: part_copy(0, s, me, lax.rem(me + 1 + i, n)).wait_recv())

    @pl.when(not_last)
    def _():
        each(n, lambda i: part_copy(1, s, me, lax.rem(me + i, n)).wait_recv())

    total = ret[0].astype(jnp.float32) + ret[1].astype(jnp.float32)
    total = total.reshape(KVH, copies, pad, 2 * HD).sum(axis=1).reshape(KVH * pad, 2 * HD)
    grads = dot(gather, total.astype(jnp.bfloat16)).astype(jnp.bfloat16)
    gk_ref[...] = grads[:, :HD]
    gv_ref[...] = grads[:, HD:]

    each(n - 1, lambda i: kv_copy(0, s, lax.rem(me + 1 + i, n), me).wait_send())
    each(n - 1, lambda i: part_copy(0, s, lax.rem(me + 1 + i, n), me).wait_send())

    @pl.when(not_last)
    def _():
        each(n, lambda i: kv_copy(1, s + 1, lax.rem(me + i, n), me).wait_send())

    @pl.when(not_first)
    def _():
        each(n, lambda i: part_copy(1, s - 1, lax.rem(me + i, n), me).wait_send())

    for store in stores:
        store.wait()


def copy_out(pieces, *refs):
    count = (len(refs) - 2) // 3
    sources, targets, held = refs[:count], refs[count:2 * count], refs[2 * count:3 * count]
    load_sem, store_sem = refs[3 * count:]
    loads, stores = [], []
    for source, target, buffer, cut in zip(sources, targets, held, pieces):
        size = source.shape[0] // cut
        for i in range(cut):
            rows = pl.ds(i * size, size)
            at = len(loads)
            loads.append(
                pltpu.make_async_copy(source.at[rows], buffer.at[rows], load_sem.at[at])
            )
            stores.append(
                pltpu.make_async_copy(buffer.at[rows], target.at[rows], store_sem.at[at])
            )
    for load in loads:
        load.start()
    for load, store in zip(loads, stores):
        load.wait()
        store.start()
    for store in stores:
        store.wait()


def per_device(n_seq, n, queries, keys, values, cotangent, mask):
    tokens, width = queries.shape
    vision = keys.shape[1]
    pad = -(-vision // 16) * 16
    heads = width // HD
    group = min(8, heads)
    half = tokens // 2
    cols = n * pad
    bf16, f32 = jnp.bfloat16, jnp.float32
    vmem = pl.BlockSpec(memory_space=pltpu.VMEM)
    hbm = pl.BlockSpec(memory_space=pltpu.HBM)
    dma = pltpu.SemaphoreType.DMA
    pieces = (4, 4, 1, 1)
    results = (
        jax.ShapeDtypeStruct((tokens, width), bf16),
        jax.ShapeDtypeStruct((tokens, width), bf16),
        jax.ShapeDtypeStruct((vision * KVH, HD), bf16),
        jax.ShapeDtypeStruct((vision * KVH, HD), bf16),
    )
    found = pl.pallas_call(
        functools.partial(kernel, n_seq, n, pad, vision, group),
        out_shape=results,
        in_specs=[hbm] * 5,
        out_specs=(hbm, hbm, vmem, vmem),
        scratch_shapes=[
            pltpu.VMEM((tokens, width), bf16),
            pltpu.VMEM((tokens, width), bf16),
            pltpu.VMEM((tokens, width), bf16),
            pltpu.VMEM((tokens, width), bf16),
            pltpu.VMEM((vision * KVH, HD), bf16),
            pltpu.VMEM((vision * KVH, HD), bf16),
            pltpu.VMEM((2, tokens), mask.dtype),
            pltpu.VMEM((2, HD, heads * half), bf16),
            pltpu.VMEM((2, HD, heads * half), bf16),
            pltpu.VMEM((KVH * pad, 2 * HD), bf16),
            pltpu.VMEM((2, cols, 2 * HD), bf16),
            pltpu.VMEM((2, cols, 2 * HD), bf16),
            pltpu.VMEM((2, cols, 2 * HD), bf16),
            pltpu.VMEM((half, 2 * cols), f32),
            pltpu.VMEM((heads * half, 2 * cols), bf16),
            pltpu.VMEM((heads * half, cols), bf16),
            pltpu.VMEM((heads * half, 2 * cols), bf16),
            pltpu.VMEM((heads * half, cols), bf16),
            dma((2, 2)),
            dma((2, 2)),
            dma((3,)),
            dma((2, n)),
            dma((2, n)),
            dma((2, n)),
            dma((2, n)),
        ],
        compiler_params=pltpu.CompilerParams(
            collective_id=0, has_side_effects=True, vmem_limit_bytes=VMEM_LIMIT
        ),
    )(
        queries,
        keys.reshape(vision * KVH, HD),
        values.reshape(vision * KVH, HD),
        cotangent,
        mask.T,
    )
    attended, grad_query, grad_keys, grad_values = pl.pallas_call(
        functools.partial(copy_out, pieces),
        out_shape=results,
        in_specs=[hbm] * 4,
        out_specs=(hbm,) * 4,
        scratch_shapes=[pltpu.VMEM(r.shape, bf16) for r in results] + [dma((sum(pieces),))] * 2,
        compiler_params=pltpu.CompilerParams(vmem_limit_bytes=VMEM_LIMIT),
    )(*found)
    shape = (1, vision, KVH, HD)
    return attended, grad_query, grad_keys.reshape(shape), grad_values.reshape(shape)


def solution(mesh):
    return jax.shard_map(
        functools.partial(per_device, mesh.shape["seq"], mesh.shape["head"]),
        mesh=mesh,
        in_specs=(
            P("seq", "head"),
            P("seq", "head", None, None),
            P("seq", "head", None, None),
            P("seq", "head"),
            P("seq", None),
        ),
        out_specs=(
            P("seq", "head"),
            P("seq", "head"),
            P("seq", "head", None, None),
            P("seq", "head", None, None),
        ),
        check_vma=False,
    )
```

```python
import functools
import math

import jax
import jax.numpy as jnp
from jax import lax
from jax.experimental import pallas as pl
from jax.experimental.pallas import tpu as pltpu
from jax.sharding import PartitionSpec as P

KVH = 8
HD = 128
NEGATIVE = -1e30
VMEM_LIMIT = 58 * 1024 * 1024
MESH = pl.DeviceIdType.MESH
SCALE = HD ** -0.5
EXP2_SCALE = SCALE * math.log2(math.e)


def dot(a, b):
    return jnp.dot(a, b, preferred_element_type=jnp.float32)


def dot_nt(a, b):
    return lax.dot_general(a, b, (((1,), (1,)), ((), ())), preferred_element_type=jnp.float32)


def each(count, body):
    if count <= 8:
        for i in range(count):
            body(i)
    else:
        lax.fori_loop(0, count, lambda i, c: (body(i), c)[1], 0)


def slot_map(pad, vision, transposed):
    shape = (vision * KVH, KVH * pad) if transposed else (KVH * pad, vision * KVH)
    slot = lax.broadcasted_iota(jnp.int32, shape, 1 if transposed else 0)
    row = lax.broadcasted_iota(jnp.int32, shape, 0 if transposed else 1)
    head, token = slot // pad, slot % pad
    return jnp.where((token < vision) & (row == token * KVH + head), 1.0, 0.0).astype(jnp.bfloat16)


def kernel(
    n_seq, n, pad, vision, group,
    q_hbm, k_hbm, v_hbm, do_hbm, mask_hbm,
    att_hbm, gq_hbm, gk_ref, gv_ref,
    q, do, att, gq, k_own, v_own, mask, qt, dot_t, stage, kv, part, ret, bias, w_lower, w_upper, gs_lower, gs_upper,
    in_sem, out_sem, small_sem, kv_send, kv_recv, part_send, part_recv,
):
    s = lax.axis_index("seq")
    me = lax.axis_index("head")
    copies = n // KVH
    tokens, width = q.shape
    heads = width // HD
    half = tokens // 2
    cols = n * pad
    not_first = s > 0
    not_last = s < n_seq - 1

    small = []
    for i, (src, dst) in enumerate(((k_hbm, k_own), (v_hbm, v_own), (mask_hbm, mask))):
        load = pltpu.make_async_copy(src, dst, small_sem.at[i])
        load.start()
        small.append(load)
    loads = []
    for i, rows in enumerate((pl.ds(half, half), pl.ds(0, half))):
        for k, (src, dst) in enumerate(((q_hbm, q), (do_hbm, do))):
            load = pltpu.make_async_copy(src.at[rows], dst.at[rows], in_sem.at[i, k])
            load.start()
            loads.append(load)

    barrier = pltpu.get_barrier_semaphore()

    def greet(block, peer):
        pl.semaphore_signal(
            barrier, inc=1, device_id={"seq": block, "head": peer}, device_id_type=MESH
        )

    each(n - 1, lambda i: greet(s, lax.rem(me + 1 + i, n)))

    @pl.when(not_first)
    def _():
        each(n, lambda i: greet(s - 1, lax.rem(me + i, n)))

    @pl.when(not_last)
    def _():
        each(n, lambda i: greet(s + 1, lax.rem(me + i, n)))

    for load in small:
        load.wait()
    spread = slot_map(pad, vision, False)
    stage[:, :HD] = dot(spread, k_own[...]).astype(jnp.bfloat16)
    stage[:, HD:] = dot(spread, v_own[...]).astype(jnp.bfloat16)

    def rows_of(index):
        return pl.ds(pl.multiple_of(index * pad, pad), pad)

    def kv_copy(b, block, peer, source):
        return pltpu.make_async_remote_copy(
            src_ref=stage.at[rows_of(peer // copies)],
            dst_ref=kv.at[b, rows_of(source)],
            send_sem=kv_send.at[b, peer],
            recv_sem=kv_recv.at[b, source],
            device_id={"seq": block, "head": peer},
            device_id_type=MESH,
        )

    def part_copy(b, block, peer, source):
        return pltpu.make_async_remote_copy(
            src_ref=part.at[b, rows_of(peer)],
            dst_ref=ret.at[b, rows_of(source)],
            send_sem=part_send.at[b, peer],
            recv_sem=part_recv.at[b, source],
            device_id={"seq": block, "head": peer},
            device_id_type=MESH,
        )

    pl.semaphore_wait(
        barrier, (n - 1) + n * not_first.astype(jnp.int32) + n * not_last.astype(jnp.int32)
    )

    each(n - 1, lambda i: kv_copy(0, s, lax.rem(me + 1 + i, n), me).start())

    @pl.when(not_last)
    def _():
        each(n, lambda i: kv_copy(1, s + 1, lax.rem(me + i, n), me).start())

    kv[0, rows_of(me), :] = stage[rows_of(me // copies), :]

    @pl.when(s == 0)
    def _():
        kv[1] = jnp.zeros(kv.shape[1:], kv.dtype)

    @pl.when(s == n_seq - 1)
    def _():
        ret[1] = jnp.zeros(ret.shape[1:], ret.dtype)

    slot_col = lax.broadcasted_iota(jnp.int32, (half, cols), 1)
    used = slot_col % pad < vision
    columns = jnp.concatenate(
        [jnp.broadcast_to(mask[i:i + 1, :half].astype(jnp.float32), (HD, half)) for i in range(2)],
        axis=0,
    ).T
    keep_own, keep_prev = columns[:, :1], columns[:, HD:HD + 1]
    bias[:, :cols] = jnp.where(used & (keep_own > 0), 0.0, NEGATIVE)
    bias[:, cols:] = jnp.where(used & (keep_prev > 0), 0.0, NEGATIVE)
    live = (keep_own + keep_prev > 0).astype(jnp.float32)
    live = jnp.concatenate([live] * group, axis=0)
    own_bias = jnp.where(used[:1], 0.0, NEGATIVE)

    for load in loads:
        load.wait()
    for h in range(heads):
        at = slice(h * HD, (h + 1) * HD)
        for b in range(2):
            to = slice(h * half, (h + 1) * half)
            rows = slice(b * half, (b + 1) * half)
            qt[b, :, to] = q[rows, at].T
            dot_t[b, :, to] = do[rows, at].T

    def stacked(ref, rows, first):
        return jnp.concatenate(
            [ref[rows, (first + i) * HD:(first + i + 1) * HD] for i in range(group)], axis=0
        )

    ones = jnp.ones((HD, HD), jnp.bfloat16)

    def attend(rows, first, keys, values, score_bias, live_rows, weight_store, grad_store):
        query = stacked(q, rows, first)
        grad = stacked(do, rows, first)
        tiles = keys.shape[0] // HD
        scores = dot_nt(query, keys) + score_bias
        yield
        grad_weights = dot_nt(grad, values)
        peak = jnp.max(scores, axis=1, keepdims=True)
        powered = jnp.exp2((scores - peak) * EXP2_SCALE)
        yield
        beside = jnp.concatenate([values, jnp.ones(values.shape, jnp.bfloat16)], axis=1)
        sums = dot(powered.astype(jnp.bfloat16), beside)
        ratio = live_rows / sums[:, HD:]
        attended = sums[:, :HD] * ratio
        delta = dot((grad.astype(jnp.float32) * attended).astype(jnp.bfloat16), ones)
        yield
        weights = powered * jnp.concatenate([ratio] * tiles, axis=1)
        grad_scores = weights * (grad_weights - jnp.concatenate([delta] * tiles, axis=1))
        for i in range(group):
            at = slice((first + i) * HD, (first + i + 1) * HD)
            att[rows, at] = attended[i * half:(i + 1) * half].astype(jnp.bfloat16)
        to = slice(first * half, (first + group) * half)
        weight_store[to, :] = weights.astype(jnp.bfloat16)
        grad_store[to, :] = grad_scores.astype(jnp.bfloat16)
        yield

    def in_step(chunks):
        stages = 4
        for time in range(stages + len(chunks) - 1):
            for place in reversed(range(len(chunks))):
                if 0 <= time - place < stages:
                    next(chunks[place])

    def put(b, key_sum, value_sum):
        part[b, :, :HD] = (key_sum * SCALE).T.astype(jnp.bfloat16)
        part[b, :, HD:] = value_sum.T.astype(jnp.bfloat16)

    def query_grads(rows, grad_store, keys):
        for first in firsts:
            grads = dot(grad_store[first * half:(first + group) * half, :], keys) * SCALE
            for i in range(group):
                at = slice((first + i) * HD, (first + i + 1) * HD)
                gq[rows, at] = grads[i * half:(i + 1) * half].astype(jnp.bfloat16)

    stores = []

    def write_out(src, dst, b, k):
        rows = pl.ds(b * half, half)
        store = pltpu.make_async_copy(src.at[rows], dst.at[rows], out_sem.at[b, k])
        store.start()
        stores.append(store)

    upper, lower = slice(half, tokens), slice(0, half)
    firsts = list(range(0, heads, group))

    each(n - 1, lambda i: kv_copy(0, s, me, lax.rem(me + 1 + i, n)).wait_recv())

    @pl.when(not_first)
    def _():
        each(n, lambda i: kv_copy(1, s, me, lax.rem(me + i, n)).wait_recv())

    both_keys = kv[:, :, :HD].reshape(2 * cols, HD)
    both_values = kv[:, :, HD:].reshape(2 * cols, HD)
    both_bias = jnp.concatenate([bias[...]] * group, axis=0)
    in_step([
        attend(lower, first, both_keys, both_values, both_bias, live, w_lower, gs_lower)
        for first in firsts
    ])
    put(1, dot(qt[0], gs_lower[:, cols:]), dot(dot_t[0], w_lower[:, cols:]))

    @pl.when(not_first)
    def _():
        each(n, lambda i: part_copy(1, s - 1, lax.rem(me + i, n), me).start())

    write_out(att, att_hbm, 0, 0)
    keys, values = kv[0, :, :HD], kv[0, :, HD:]
    in_step([
        attend(upper, first, keys, values, own_bias, 1.0, w_upper, gs_upper) for first in firsts
    ])
    put(
        0,
        dot(qt[0], gs_lower[:, :cols]) + dot(qt[1], gs_upper[...]),
        dot(dot_t[0], w_lower[:, :cols]) + dot(dot_t[1], w_upper[...]),
    )
    each(n - 1, lambda i: part_copy(0, s, lax.rem(me + 1 + i, n), me).start())
    ret[0, rows_of(me), :] = part[0, rows_of(me), :]
    write_out(att, att_hbm, 1, 0)
    query_grads(upper, gs_upper, keys)
    write_out(gq, gq_hbm, 1, 1)
    query_grads(lower, gs_lower, both_keys)
    write_out(gq, gq_hbm, 0, 1)

    gather = slot_map(pad, vision, True)
    each(n - 1, lambda i: part_copy(0, s, me, lax.rem(me + 1 + i, n)).wait_recv())

    @pl.when(not_last)
    def _():
        each(n, lambda i: part_copy(1, s, me, lax.rem(me + i, n)).wait_recv())

    total = ret[0].astype(jnp.float32) + ret[1].astype(jnp.float32)
    total = total.reshape(KVH, copies, pad, 2 * HD).sum(axis=1).reshape(KVH * pad, 2 * HD)
    grads = dot(gather, total.astype(jnp.bfloat16)).astype(jnp.bfloat16)
    gk_ref[...] = grads[:, :HD]
    gv_ref[...] = grads[:, HD:]

    each(n - 1, lambda i: kv_copy(0, s, lax.rem(me + 1 + i, n), me).wait_send())
    each(n - 1, lambda i: part_copy(0, s, lax.rem(me + 1 + i, n), me).wait_send())

    @pl.when(not_last)
    def _():
        each(n, lambda i: kv_copy(1, s + 1, lax.rem(me + i, n), me).wait_send())

    @pl.when(not_first)
    def _():
        each(n, lambda i: part_copy(1, s - 1, lax.rem(me + i, n), me).wait_send())

    for store in stores:
        store.wait()


def copy_out(pieces, *refs):
    count = (len(refs) - 2) // 3
    sources, targets, held = refs[:count], refs[count:2 * count], refs[2 * count:3 * count]
    load_sem, store_sem = refs[3 * count:]
    loads, stores = [], []
    for source, target, buffer, cut in zip(sources, targets, held, pieces):
        size = source.shape[0] // cut
        for i in range(cut):
            rows = pl.ds(i * size, size)
            at = len(loads)
            loads.append(
                pltpu.make_async_copy(source.at[rows], buffer.at[rows], load_sem.at[at])
            )
            stores.append(
                pltpu.make_async_copy(buffer.at[rows], target.at[rows], store_sem.at[at])
            )
    for load in loads:
        load.start()
    for load, store in zip(loads, stores):
        load.wait()
        store.start()
    for store in stores:
        store.wait()


def per_device(n_seq, n, queries, keys, values, cotangent, mask):
    tokens, width = queries.shape
    vision = keys.shape[1]
    pad = -(-vision // 16) * 16
    heads = width // HD
    group = min(4, heads)
    half = tokens // 2
    cols = n * pad
    bf16, f32 = jnp.bfloat16, jnp.float32
    vmem = pl.BlockSpec(memory_space=pltpu.VMEM)
    hbm = pl.BlockSpec(memory_space=pltpu.HBM)
    dma = pltpu.SemaphoreType.DMA
    pieces = (1, 1, 1, 1)
    results = (
        jax.ShapeDtypeStruct((tokens, width), bf16),
        jax.ShapeDtypeStruct((tokens, width), bf16),
        jax.ShapeDtypeStruct((vision * KVH, HD), bf16),
        jax.ShapeDtypeStruct((vision * KVH, HD), bf16),
    )
    found = pl.pallas_call(
        functools.partial(kernel, n_seq, n, pad, vision, group),
        out_shape=results,
        in_specs=[hbm] * 5,
        out_specs=(hbm, hbm, vmem, vmem),
        scratch_shapes=[
            pltpu.VMEM((tokens, width), bf16),
            pltpu.VMEM((tokens, width), bf16),
            pltpu.VMEM((tokens, width), bf16),
            pltpu.VMEM((tokens, width), bf16),
            pltpu.VMEM((vision * KVH, HD), bf16),
            pltpu.VMEM((vision * KVH, HD), bf16),
            pltpu.VMEM((2, tokens), mask.dtype),
            pltpu.VMEM((2, HD, heads * half), bf16),
            pltpu.VMEM((2, HD, heads * half), bf16),
            pltpu.VMEM((KVH * pad, 2 * HD), bf16),
            pltpu.VMEM((2, cols, 2 * HD), bf16),
            pltpu.VMEM((2, cols, 2 * HD), bf16),
            pltpu.VMEM((2, cols, 2 * HD), bf16),
            pltpu.VMEM((half, 2 * cols), f32),
            pltpu.VMEM((heads * half, 2 * cols), bf16),
            pltpu.VMEM((heads * half, cols), bf16),
            pltpu.VMEM((heads * half, 2 * cols), bf16),
            pltpu.VMEM((heads * half, cols), bf16),
            dma((2, 2)),
            dma((2, 2)),
            dma((3,)),
            dma((2, n)),
            dma((2, n)),
            dma((2, n)),
            dma((2, n)),
        ],
        compiler_params=pltpu.CompilerParams(
            collective_id=0, has_side_effects=True, vmem_limit_bytes=VMEM_LIMIT
        ),
    )(
        queries,
        keys.reshape(vision * KVH, HD),
        values.reshape(vision * KVH, HD),
        cotangent,
        mask.T,
    )
    attended, grad_query, grad_keys, grad_values = pl.pallas_call(
        functools.partial(copy_out, pieces),
        out_shape=results,
        in_specs=[hbm] * 4,
        out_specs=(hbm,) * 4,
        scratch_shapes=[pltpu.VMEM(r.shape, bf16) for r in results] + [dma((sum(pieces),))] * 2,
        compiler_params=pltpu.CompilerParams(vmem_limit_bytes=VMEM_LIMIT),
    )(*found)
    shape = (1, vision, KVH, HD)
    return attended, grad_query, grad_keys.reshape(shape), grad_values.reshape(shape)


def solution(mesh):
    return jax.shard_map(
        functools.partial(per_device, mesh.shape["seq"], mesh.shape["head"]),
        mesh=mesh,
        in_specs=(
            P("seq", "head"),
            P("seq", "head", None, None),
            P("seq", "head", None, None),
            P("seq", "head"),
            P("seq", None),
        ),
        out_specs=(
            P("seq", "head"),
            P("seq", "head"),
            P("seq", "head", None, None),
            P("seq", "head", None, None),
        ),
        check_vma=False,
    )
```

```python
import functools
import math

import jax
import jax.numpy as jnp
from jax import lax
from jax.experimental import pallas as pl
from jax.experimental.pallas import tpu as pltpu
from jax.sharding import PartitionSpec as P

KVH = 8
HD = 128
NEGATIVE = -1e30
VMEM_LIMIT = 58 * 1024 * 1024
MESH = pl.DeviceIdType.MESH
SCALE = HD ** -0.5
EXP2_SCALE = SCALE * math.log2(math.e)


def dot(a, b):
    return jnp.dot(a, b, preferred_element_type=jnp.float32)


def dot_nt(a, b):
    return lax.dot_general(a, b, (((1,), (1,)), ((), ())), preferred_element_type=jnp.float32)


def each(count, body):
    if count <= 8:
        for i in range(count):
            body(i)
    else:
        lax.fori_loop(0, count, lambda i, c: (body(i), c)[1], 0)


def slot_map(pad, vision, transposed):
    shape = (vision * KVH, KVH * pad) if transposed else (KVH * pad, vision * KVH)
    slot = lax.broadcasted_iota(jnp.int32, shape, 1 if transposed else 0)
    row = lax.broadcasted_iota(jnp.int32, shape, 0 if transposed else 1)
    head, token = slot // pad, slot % pad
    return jnp.where((token < vision) & (row == token * KVH + head), 1.0, 0.0).astype(jnp.bfloat16)


def kernel(
    n_seq, n, pad, vision, group,
    q_hbm, k_hbm, v_hbm, do_hbm, mask_hbm,
    att_hbm, gq_hbm, ret,
    q, do, att, gq, k_own, v_own, mask, qt, dot_t, stage, kv, part, bias, w_lower, w_upper, gs_lower, gs_upper,
    in_sem, out_sem, small_sem, kv_send, kv_recv, part_send, part_recv, kept_sem,
):
    s = lax.axis_index("seq")
    me = lax.axis_index("head")
    copies = n // KVH
    tokens, width = q.shape
    heads = width // HD
    half = tokens // 2
    cols = n * pad
    not_first = s > 0
    not_last = s < n_seq - 1

    small = []
    for i, (src, dst) in enumerate(((k_hbm, k_own), (v_hbm, v_own), (mask_hbm, mask))):
        load = pltpu.make_async_copy(src, dst, small_sem.at[i])
        load.start()
        small.append(load)
    loads = []
    for i, rows in enumerate((pl.ds(half, half), pl.ds(0, half))):
        for k, (src, dst) in enumerate(((q_hbm, q), (do_hbm, do))):
            load = pltpu.make_async_copy(src.at[rows], dst.at[rows], in_sem.at[i, k])
            load.start()
            loads.append(load)

    barrier = pltpu.get_barrier_semaphore()

    def greet(block, peer):
        pl.semaphore_signal(
            barrier, inc=1, device_id={"seq": block, "head": peer}, device_id_type=MESH
        )

    each(n - 1, lambda i: greet(s, lax.rem(me + 1 + i, n)))

    @pl.when(not_first)
    def _():
        each(n, lambda i: greet(s - 1, lax.rem(me + i, n)))

    @pl.when(not_last)
    def _():
        each(n, lambda i: greet(s + 1, lax.rem(me + i, n)))

    for load in small:
        load.wait()
    spread = slot_map(pad, vision, False)
    stage[:, :HD] = dot(spread, k_own[...]).astype(jnp.bfloat16)
    stage[:, HD:] = dot(spread, v_own[...]).astype(jnp.bfloat16)

    def rows_of(index):
        return pl.ds(pl.multiple_of(index * pad, pad), pad)

    def kv_copy(b, block, peer, source):
        return pltpu.make_async_remote_copy(
            src_ref=stage.at[rows_of(peer // copies)],
            dst_ref=kv.at[b, rows_of(source)],
            send_sem=kv_send.at[b, peer],
            recv_sem=kv_recv.at[b, source],
            device_id={"seq": block, "head": peer},
            device_id_type=MESH,
        )

    def part_copy(b, block, peer, source):
        return pltpu.make_async_remote_copy(
            src_ref=part.at[b, rows_of(peer)],
            dst_ref=ret.at[b, rows_of(source)],
            send_sem=part_send.at[b, peer],
            recv_sem=part_recv.at[b, source],
            device_id={"seq": block, "head": peer},
            device_id_type=MESH,
        )

    pl.semaphore_wait(
        barrier, (n - 1) + n * not_first.astype(jnp.int32) + n * not_last.astype(jnp.int32)
    )


    @pl.when(not_last)
    def _():
        each(n, lambda i: kv_copy(1, s + 1, lax.rem(me + i, n), me).start())

    each(n - 1, lambda i: kv_copy(0, s, lax.rem(me + 1 + i, n), me).start())
    kv[0, rows_of(me), :] = stage[rows_of(me // copies), :]

    @pl.when(s == 0)
    def _():
        kv[1] = jnp.zeros(kv.shape[1:], kv.dtype)

    slot_col = lax.broadcasted_iota(jnp.int32, (half, cols), 1)
    used = slot_col % pad < vision
    columns = jnp.concatenate(
        [jnp.broadcast_to(mask[i:i + 1, :half].astype(jnp.float32), (HD, half)) for i in range(2)],
        axis=0,
    ).T
    keep_own, keep_prev = columns[:, :1], columns[:, HD:HD + 1]
    bias[:, :cols] = jnp.where(used & (keep_own > 0), 0.0, NEGATIVE)
    bias[:, cols:] = jnp.where(used & (keep_prev > 0), 0.0, NEGATIVE)
    live = (keep_own + keep_prev > 0).astype(jnp.float32)
    live = jnp.concatenate([live] * group, axis=0)
    own_bias = jnp.where(used[:1], 0.0, NEGATIVE)

    for load in loads:
        load.wait()
    for h in range(heads):
        at = slice(h * HD, (h + 1) * HD)
        for b in range(2):
            to = slice(h * half, (h + 1) * half)
            rows = slice(b * half, (b + 1) * half)
            qt[b, :, to] = q[rows, at].T
            dot_t[b, :, to] = do[rows, at].T

    def stacked(ref, rows, first):
        return jnp.concatenate(
            [ref[rows, (first + i) * HD:(first + i + 1) * HD] for i in range(group)], axis=0
        )

    ones = jnp.ones((HD, HD), jnp.bfloat16)

    def attend(rows, first, keys, values, score_bias, live_rows, weight_store, grad_store):
        query = stacked(q, rows, first)
        grad = stacked(do, rows, first)
        tiles = keys.shape[0] // HD
        scores = dot_nt(query, keys) + score_bias
        yield
        grad_weights = dot_nt(grad, values)
        peak = jnp.max(scores, axis=1, keepdims=True)
        powered = jnp.exp2((scores - peak) * EXP2_SCALE)
        yield
        beside = jnp.concatenate([values, jnp.ones(values.shape, jnp.bfloat16)], axis=1)
        sums = dot(powered.astype(jnp.bfloat16), beside)
        ratio = live_rows / sums[:, HD:]
        attended = sums[:, :HD] * ratio
        delta = dot((grad.astype(jnp.float32) * attended).astype(jnp.bfloat16), ones)
        yield
        weights = powered * jnp.concatenate([ratio] * tiles, axis=1)
        grad_scores = weights * (grad_weights - jnp.concatenate([delta] * tiles, axis=1))
        for i in range(group):
            at = slice((first + i) * HD, (first + i + 1) * HD)
            att[rows, at] = attended[i * half:(i + 1) * half].astype(jnp.bfloat16)
        to = slice(first * half, (first + group) * half)
        weight_store[to, :] = weights.astype(jnp.bfloat16)
        grad_store[to, :] = grad_scores.astype(jnp.bfloat16)
        yield

    def in_step(chunks):
        stages = 4
        for time in range(stages + len(chunks) - 1):
            for place in reversed(range(len(chunks))):
                if 0 <= time - place < stages:
                    next(chunks[place])

    def put(b, key_sum, value_sum):
        part[b, :, :HD] = (key_sum * SCALE).T.astype(jnp.bfloat16)
        part[b, :, HD:] = value_sum.T.astype(jnp.bfloat16)

    def query_grads(rows, grad_store, keys):
        for first in firsts:
            grads = dot(grad_store[first * half:(first + group) * half, :], keys) * SCALE
            for i in range(group):
                at = slice((first + i) * HD, (first + i + 1) * HD)
                gq[rows, at] = grads[i * half:(i + 1) * half].astype(jnp.bfloat16)

    stores = []

    def write_out(src, dst, b, k):
        rows = pl.ds(b * half, half)
        store = pltpu.make_async_copy(src.at[rows], dst.at[rows], out_sem.at[b, k])
        store.start()
        stores.append(store)

    upper, lower = slice(half, tokens), slice(0, half)
    firsts = list(range(0, heads, group))

    each(n - 1, lambda i: kv_copy(0, s, me, lax.rem(me + 1 + i, n)).wait_recv())

    @pl.when(not_first)
    def _():
        each(n, lambda i: kv_copy(1, s, me, lax.rem(me + i, n)).wait_recv())

    both_keys = kv[:, :, :HD].reshape(2 * cols, HD)
    both_values = kv[:, :, HD:].reshape(2 * cols, HD)
    both_bias = jnp.concatenate([bias[...]] * group, axis=0)
    in_step([
        attend(lower, first, both_keys, both_values, both_bias, live, w_lower, gs_lower)
        for first in firsts
    ])
    put(1, dot(qt[0], gs_lower[:, cols:]), dot(dot_t[0], w_lower[:, cols:]))

    @pl.when(not_first)
    def _():
        each(n, lambda i: part_copy(1, s - 1, lax.rem(me + i, n), me).start())

    write_out(att, att_hbm, 0, 0)
    keys, values = kv[0, :, :HD], kv[0, :, HD:]
    in_step([
        attend(upper, first, keys, values, own_bias, 1.0, w_upper, gs_upper) for first in firsts
    ])
    put(
        0,
        dot(qt[0], gs_lower[:, :cols]) + dot(qt[1], gs_upper[...]),
        dot(dot_t[0], w_lower[:, :cols]) + dot(dot_t[1], w_upper[...]),
    )
    each(n - 1, lambda i: part_copy(0, s, lax.rem(me + 1 + i, n), me).start())
    kept = pltpu.make_async_copy(part.at[0, rows_of(me)], ret.at[0, rows_of(me)], kept_sem)
    kept.start()
    write_out(att, att_hbm, 1, 0)
    query_grads(upper, gs_upper, keys)
    write_out(gq, gq_hbm, 1, 1)
    query_grads(lower, gs_lower, both_keys)
    write_out(gq, gq_hbm, 0, 1)

    each(n - 1, lambda i: part_copy(0, s, me, lax.rem(me + 1 + i, n)).wait_recv())

    @pl.when(not_last)
    def _():
        each(n, lambda i: part_copy(1, s, me, lax.rem(me + i, n)).wait_recv())

    kept.wait()
    each(n - 1, lambda i: kv_copy(0, s, lax.rem(me + 1 + i, n), me).wait_send())
    each(n - 1, lambda i: part_copy(0, s, lax.rem(me + 1 + i, n), me).wait_send())

    @pl.when(not_last)
    def _():
        each(n, lambda i: kv_copy(1, s + 1, lax.rem(me + i, n), me).wait_send())

    @pl.when(not_first)
    def _():
        each(n, lambda i: part_copy(1, s - 1, lax.rem(me + i, n), me).wait_send())

    for store in stores:
        store.wait()


def finish(
    n_seq, pad, vision, att_in, gq_in, ret_in, att_out, gq_out, gk_out, gv_out,
    att, gq, ret, gk, gv, load_sem, store_sem,
):
    not_last = lax.axis_index("seq") < n_seq - 1
    own = pltpu.make_async_copy(ret_in.at[0], ret.at[0], load_sem.at[0])
    following = pltpu.make_async_copy(ret_in.at[1], ret.at[1], load_sem.at[1])
    own.start()
    pl.when(not_last)(following.start)
    loads, stores = [], []
    for i, (source, buffer, target) in enumerate(((att_in, att, att_out), (gq_in, gq, gq_out))):
        loads.append(pltpu.make_async_copy(source, buffer, load_sem.at[2 + i]))
        stores.append(pltpu.make_async_copy(buffer, target, store_sem.at[i]))
    for load in loads:
        load.start()

    @pl.when(jnp.logical_not(not_last))
    def _():
        ret[1] = jnp.zeros(ret.shape[1:], ret.dtype)

    gather = slot_map(pad, vision, True)
    own.wait()
    pl.when(not_last)(following.wait)
    for load, store in zip(loads, stores):
        load.wait()
        store.start()
    total = ret[0].astype(jnp.float32) + ret[1].astype(jnp.float32)
    copies = ret.shape[1] // (KVH * pad)
    total = total.reshape(KVH, copies, pad, 2 * HD).sum(axis=1).reshape(KVH * pad, 2 * HD)
    grads = dot(gather, total.astype(jnp.bfloat16)).astype(jnp.bfloat16)
    for i, (buffer, target) in enumerate(((gk, gk_out), (gv, gv_out))):
        buffer[...] = grads[:, i * HD:(i + 1) * HD]
        stores.append(pltpu.make_async_copy(buffer, target, store_sem.at[2 + i]))
        stores[-1].start()
    for store in stores:
        store.wait()


def per_device(n_seq, n, queries, keys, values, cotangent, mask):
    tokens, width = queries.shape
    vision = keys.shape[1]
    pad = -(-vision // 16) * 16
    heads = width // HD
    group = min(4, heads)
    half = tokens // 2
    cols = n * pad
    bf16, f32 = jnp.bfloat16, jnp.float32
    hbm = pl.BlockSpec(memory_space=pltpu.HBM)
    dma = pltpu.SemaphoreType.DMA
    results = (
        jax.ShapeDtypeStruct((tokens, width), bf16),
        jax.ShapeDtypeStruct((tokens, width), bf16),
        jax.ShapeDtypeStruct((vision * KVH, HD), bf16),
        jax.ShapeDtypeStruct((vision * KVH, HD), bf16),
    )
    found = pl.pallas_call(
        functools.partial(kernel, n_seq, n, pad, vision, group),
        out_shape=results[:2] + (jax.ShapeDtypeStruct((2, cols, 2 * HD), bf16),),
        in_specs=[hbm] * 5,
        out_specs=(hbm,) * 3,
        scratch_shapes=[
            pltpu.VMEM((tokens, width), bf16),
            pltpu.VMEM((tokens, width), bf16),
            pltpu.VMEM((tokens, width), bf16),
            pltpu.VMEM((tokens, width), bf16),
            pltpu.VMEM((vision * KVH, HD), bf16),
            pltpu.VMEM((vision * KVH, HD), bf16),
            pltpu.VMEM((2, tokens), mask.dtype),
            pltpu.VMEM((2, HD, heads * half), bf16),
            pltpu.VMEM((2, HD, heads * half), bf16),
            pltpu.VMEM((KVH * pad, 2 * HD), bf16),
            pltpu.VMEM((2, cols, 2 * HD), bf16),
            pltpu.VMEM((2, cols, 2 * HD), bf16),
            pltpu.VMEM((half, 2 * cols), f32),
            pltpu.VMEM((heads * half, 2 * cols), bf16),
            pltpu.VMEM((heads * half, cols), bf16),
            pltpu.VMEM((heads * half, 2 * cols), bf16),
            pltpu.VMEM((heads * half, cols), bf16),
            dma((2, 2)),
            dma((2, 2)),
            dma((3,)),
            dma((2, n)),
            dma((2, n)),
            dma((2, n)),
            dma((2, n)),
            dma,
        ],
        compiler_params=pltpu.CompilerParams(
            collective_id=0, has_side_effects=True, vmem_limit_bytes=VMEM_LIMIT
        ),
    )(
        queries,
        keys.reshape(vision * KVH, HD),
        values.reshape(vision * KVH, HD),
        cotangent,
        mask.T,
    )
    attended, grad_query, grad_keys, grad_values = pl.pallas_call(
        functools.partial(finish, n_seq, pad, vision),
        out_shape=results,
        in_specs=[hbm] * 3,
        out_specs=(hbm,) * 4,
        scratch_shapes=[
            pltpu.VMEM((tokens, width), bf16),
            pltpu.VMEM((tokens, width), bf16),
            pltpu.VMEM((2, cols, 2 * HD), bf16),
            pltpu.VMEM((vision * KVH, HD), bf16),
            pltpu.VMEM((vision * KVH, HD), bf16),
            dma((4,)),
            dma((4,)),
        ],
        compiler_params=pltpu.CompilerParams(vmem_limit_bytes=VMEM_LIMIT),
    )(*found)
    shape = (1, vision, KVH, HD)
    return attended, grad_query, grad_keys.reshape(shape), grad_values.reshape(shape)


def solution(mesh):
    return jax.shard_map(
        functools.partial(per_device, mesh.shape["seq"], mesh.shape["head"]),
        mesh=mesh,
        in_specs=(
            P("seq", "head"),
            P("seq", "head", None, None),
            P("seq", "head", None, None),
            P("seq", "head"),
            P("seq", None),
        ),
        out_specs=(
            P("seq", "head"),
            P("seq", "head"),
            P("seq", "head", None, None),
            P("seq", "head", None, None),
        ),
        check_vma=False,
    )
```

```python
import functools
import math

import jax
import jax.numpy as jnp
from jax import lax
from jax.experimental import pallas as pl
from jax.experimental.pallas import tpu as pltpu
from jax.sharding import PartitionSpec as P

KVH = 8
HD = 128
NEGATIVE = -1e30
VMEM_LIMIT = 58 * 1024 * 1024
MESH = pl.DeviceIdType.MESH
SCALE = HD ** -0.5
EXP2_SCALE = SCALE * math.log2(math.e)


def dot(a, b):
    return jnp.dot(a, b, preferred_element_type=jnp.float32)


def dot_nt(a, b):
    return lax.dot_general(a, b, (((1,), (1,)), ((), ())), preferred_element_type=jnp.float32)


def each(count, body):
    if count <= 8:
        for i in range(count):
            body(i)
    else:
        lax.fori_loop(0, count, lambda i, c: (body(i), c)[1], 0)


def slot_map(pad, vision, transposed):
    shape = (vision * KVH, KVH * pad) if transposed else (KVH * pad, vision * KVH)
    slot = lax.broadcasted_iota(jnp.int32, shape, 1 if transposed else 0)
    row = lax.broadcasted_iota(jnp.int32, shape, 0 if transposed else 1)
    head, token = slot // pad, slot % pad
    return jnp.where((token < vision) & (row == token * KVH + head), 1.0, 0.0).astype(jnp.bfloat16)


def kernel(
    n_seq, n, pad, vision, group,
    q_hbm, k_hbm, v_hbm, do_hbm, mask_hbm,
    att_hbm, gq_hbm, ret,
    q, do, att, gq, k_own, v_own, mask, qt, dot_t, stage, kv, part, bias, w_lower, w_upper, gs_lower, gs_upper,
    in_sem, out_sem, small_sem, kv_send, kv_recv, part_send, part_recv, kept_sem,
):
    s = lax.axis_index("seq")
    me = lax.axis_index("head")
    copies = n // KVH
    tokens, width = q.shape
    heads = width // HD
    half = tokens // 2
    cols = n * pad
    not_first = s > 0
    not_last = s < n_seq - 1

    small = []
    for i, (src, dst) in enumerate(((k_hbm, k_own), (v_hbm, v_own), (mask_hbm, mask))):
        load = pltpu.make_async_copy(src, dst, small_sem.at[i])
        load.start()
        small.append(load)
    loads = []
    for i, rows in enumerate((pl.ds(half, half), pl.ds(0, half))):
        for k, (src, dst) in enumerate(((q_hbm, q), (do_hbm, do))):
            load = pltpu.make_async_copy(src.at[rows], dst.at[rows], in_sem.at[i, k])
            load.start()
            loads.append(load)

    barrier = pltpu.get_barrier_semaphore()

    def greet(block, peer):
        pl.semaphore_signal(
            barrier, inc=1, device_id={"seq": block, "head": peer}, device_id_type=MESH
        )

    each(n - 1, lambda i: greet(s, lax.rem(me + 1 + i, n)))

    @pl.when(not_first)
    def _():
        each(n, lambda i: greet(s - 1, lax.rem(me + i, n)))

    @pl.when(not_last)
    def _():
        each(n, lambda i: greet(s + 1, lax.rem(me + i, n)))

    for load in small:
        load.wait()
    spread = slot_map(pad, vision, False)
    stage[:, :HD] = dot(spread, k_own[...]).astype(jnp.bfloat16)
    stage[:, HD:] = dot(spread, v_own[...]).astype(jnp.bfloat16)

    def rows_of(index):
        return pl.ds(pl.multiple_of(index * pad, pad), pad)

    def kv_copy(b, block, peer, source):
        return pltpu.make_async_remote_copy(
            src_ref=stage.at[rows_of(peer // copies)],
            dst_ref=kv.at[b, rows_of(source)],
            send_sem=kv_send.at[b, peer],
            recv_sem=kv_recv.at[b, source],
            device_id={"seq": block, "head": peer},
            device_id_type=MESH,
        )

    def part_copy(b, block, peer, source):
        return pltpu.make_async_remote_copy(
            src_ref=part.at[b, rows_of(peer)],
            dst_ref=ret.at[b, rows_of(source)],
            send_sem=part_send.at[b, peer],
            recv_sem=part_recv.at[b, source],
            device_id={"seq": block, "head": peer},
            device_id_type=MESH,
        )

    pl.semaphore_wait(
        barrier, (n - 1) + n * not_first.astype(jnp.int32) + n * not_last.astype(jnp.int32)
    )


    @pl.when(not_last)
    def _():
        each(n, lambda i: kv_copy(1, s + 1, lax.rem(me + i, n), me).start())

    each(n - 1, lambda i: kv_copy(0, s, lax.rem(me + 1 + i, n), me).start())
    kv[0, rows_of(me), :] = stage[rows_of(me // copies), :]

    @pl.when(s == 0)
    def _():
        kv[1] = jnp.zeros(kv.shape[1:], kv.dtype)

    slot_col = lax.broadcasted_iota(jnp.int32, (half, cols), 1)
    used = slot_col % pad < vision
    columns = jnp.concatenate(
        [jnp.broadcast_to(mask[i:i + 1, :half].astype(jnp.float32), (HD, half)) for i in range(2)],
        axis=0,
    ).T
    keep_own, keep_prev = columns[:, :1], columns[:, HD:HD + 1]
    bias[:, :cols] = jnp.where(used & (keep_own > 0), 0.0, NEGATIVE)
    bias[:, cols:] = jnp.where(used & (keep_prev > 0), 0.0, NEGATIVE)
    live = (keep_own + keep_prev > 0).astype(jnp.float32)
    live = jnp.concatenate([live] * group, axis=0)
    own_bias = jnp.where(used[:1], 0.0, NEGATIVE)

    for load in loads:
        load.wait()

    def turn(b):
        for h in range(heads):
            at = slice(h * HD, (h + 1) * HD)
            to = slice(h * half, (h + 1) * half)
            rows = slice(b * half, (b + 1) * half)
            qt[b, :, to] = q[rows, at].T
            dot_t[b, :, to] = do[rows, at].T

    turn(0)

    def stacked(ref, rows, first):
        return jnp.concatenate(
            [ref[rows, (first + i) * HD:(first + i + 1) * HD] for i in range(group)], axis=0
        )

    ones = jnp.ones((HD, HD), jnp.bfloat16)

    def attend(rows, first, keys, values, score_bias, live_rows, weight_store, grad_store):
        query = stacked(q, rows, first)
        grad = stacked(do, rows, first)
        tiles = keys.shape[0] // HD
        scores = dot_nt(query, keys) + score_bias
        yield
        grad_weights = dot_nt(grad, values)
        peak = jnp.max(scores, axis=1, keepdims=True)
        powered = jnp.exp2((scores - peak) * EXP2_SCALE)
        yield
        beside = jnp.concatenate([values, jnp.ones(values.shape, jnp.bfloat16)], axis=1)
        sums = dot(powered.astype(jnp.bfloat16), beside)
        ratio = live_rows / sums[:, HD:]
        attended = sums[:, :HD] * ratio
        delta = dot((grad.astype(jnp.float32) * attended).astype(jnp.bfloat16), ones)
        yield
        weights = powered * jnp.concatenate([ratio] * tiles, axis=1)
        grad_scores = weights * (grad_weights - jnp.concatenate([delta] * tiles, axis=1))
        for i in range(group):
            at = slice((first + i) * HD, (first + i + 1) * HD)
            att[rows, at] = attended[i * half:(i + 1) * half].astype(jnp.bfloat16)
        to = slice(first * half, (first + group) * half)
        weight_store[to, :] = weights.astype(jnp.bfloat16)
        grad_store[to, :] = grad_scores.astype(jnp.bfloat16)
        yield

    def in_step(chunks):
        stages = 4
        for time in range(stages + len(chunks) - 1):
            for place in reversed(range(len(chunks))):
                if 0 <= time - place < stages:
                    next(chunks[place])

    def put(b, key_sum, value_sum):
        part[b, :, :HD] = (key_sum * SCALE).astype(jnp.bfloat16).T
        part[b, :, HD:] = value_sum.astype(jnp.bfloat16).T

    def query_grads(rows, grad_store, keys):
        for first in firsts:
            grads = dot(grad_store[first * half:(first + group) * half, :], keys) * SCALE
            for i in range(group):
                at = slice((first + i) * HD, (first + i + 1) * HD)
                gq[rows, at] = grads[i * half:(i + 1) * half].astype(jnp.bfloat16)

    stores = []

    def write_out(src, dst, b, k):
        rows = pl.ds(b * half, half)
        store = pltpu.make_async_copy(src.at[rows], dst.at[rows], out_sem.at[b, k])
        store.start()
        stores.append(store)

    upper, lower = slice(half, tokens), slice(0, half)
    firsts = list(range(0, heads, group))

    each(n - 1, lambda i: kv_copy(0, s, me, lax.rem(me + 1 + i, n)).wait_recv())

    @pl.when(not_first)
    def _():
        each(n, lambda i: kv_copy(1, s, me, lax.rem(me + i, n)).wait_recv())

    both_keys = kv[:, :, :HD].reshape(2 * cols, HD)
    both_values = kv[:, :, HD:].reshape(2 * cols, HD)
    both_bias = jnp.concatenate([bias[...]] * group, axis=0)
    in_step([
        attend(lower, first, both_keys, both_values, both_bias, live, w_lower, gs_lower)
        for first in firsts
    ])
    put(1, dot(qt[0], gs_lower[:, cols:]), dot(dot_t[0], w_lower[:, cols:]))

    @pl.when(not_first)
    def _():
        each(n, lambda i: part_copy(1, s - 1, lax.rem(me + i, n), me).start())

    write_out(att, att_hbm, 0, 0)
    turn(1)
    keys, values = kv[0, :, :HD], kv[0, :, HD:]
    in_step([
        attend(upper, first, keys, values, own_bias, 1.0, w_upper, gs_upper) for first in firsts
    ])
    put(
        0,
        dot(qt[0], gs_lower[:, :cols]) + dot(qt[1], gs_upper[...]),
        dot(dot_t[0], w_lower[:, :cols]) + dot(dot_t[1], w_upper[...]),
    )
    each(n - 1, lambda i: part_copy(0, s, lax.rem(me + 1 + i, n), me).start())
    kept = pltpu.make_async_copy(part.at[0, rows_of(me)], ret.at[0, rows_of(me)], kept_sem)
    kept.start()
    write_out(att, att_hbm, 1, 0)
    query_grads(upper, gs_upper, keys)
    write_out(gq, gq_hbm, 1, 1)
    query_grads(lower, gs_lower, both_keys)
    write_out(gq, gq_hbm, 0, 1)

    each(n - 1, lambda i: part_copy(0, s, me, lax.rem(me + 1 + i, n)).wait_recv())

    @pl.when(not_last)
    def _():
        each(n, lambda i: part_copy(1, s, me, lax.rem(me + i, n)).wait_recv())

    kept.wait()
    each(n - 1, lambda i: kv_copy(0, s, lax.rem(me + 1 + i, n), me).wait_send())
    each(n - 1, lambda i: part_copy(0, s, lax.rem(me + 1 + i, n), me).wait_send())

    @pl.when(not_last)
    def _():
        each(n, lambda i: kv_copy(1, s + 1, lax.rem(me + i, n), me).wait_send())

    @pl.when(not_first)
    def _():
        each(n, lambda i: part_copy(1, s - 1, lax.rem(me + i, n), me).wait_send())

    for store in stores:
        store.wait()


def finish(
    n_seq, pad, vision, att_in, gq_in, ret_in, att_out, gq_out, gk_out, gv_out,
    att, gq, ret, gk, gv, load_sem, store_sem,
):
    not_last = lax.axis_index("seq") < n_seq - 1
    own = pltpu.make_async_copy(ret_in.at[0], ret.at[0], load_sem.at[0])
    following = pltpu.make_async_copy(ret_in.at[1], ret.at[1], load_sem.at[1])
    own.start()
    pl.when(not_last)(following.start)
    loads, stores = [], []
    for i, (source, buffer, target) in enumerate(((att_in, att, att_out), (gq_in, gq, gq_out))):
        loads.append(pltpu.make_async_copy(source, buffer, load_sem.at[2 + i]))
        stores.append(pltpu.make_async_copy(buffer, target, store_sem.at[i]))
    for load in loads:
        load.start()

    @pl.when(jnp.logical_not(not_last))
    def _():
        ret[1] = jnp.zeros(ret.shape[1:], ret.dtype)

    gather = slot_map(pad, vision, True)
    own.wait()
    pl.when(not_last)(following.wait)
    for load, store in zip(loads, stores):
        load.wait()
        store.start()
    total = ret[0].astype(jnp.float32) + ret[1].astype(jnp.float32)
    copies = ret.shape[1] // (KVH * pad)
    total = total.reshape(KVH, copies, pad, 2 * HD).sum(axis=1).reshape(KVH * pad, 2 * HD)
    grads = dot(gather, total.astype(jnp.bfloat16)).astype(jnp.bfloat16)
    for i, (buffer, target) in enumerate(((gk, gk_out), (gv, gv_out))):
        buffer[...] = grads[:, i * HD:(i + 1) * HD]
        stores.append(pltpu.make_async_copy(buffer, target, store_sem.at[2 + i]))
        stores[-1].start()
    for store in stores:
        store.wait()


def per_device(n_seq, n, queries, keys, values, cotangent, mask):
    tokens, width = queries.shape
    vision = keys.shape[1]
    pad = -(-vision // 16) * 16
    heads = width // HD
    group = min(4, heads)
    half = tokens // 2
    cols = n * pad
    bf16, f32 = jnp.bfloat16, jnp.float32
    hbm = pl.BlockSpec(memory_space=pltpu.HBM)
    dma = pltpu.SemaphoreType.DMA
    results = (
        jax.ShapeDtypeStruct((tokens, width), bf16),
        jax.ShapeDtypeStruct((tokens, width), bf16),
        jax.ShapeDtypeStruct((vision * KVH, HD), bf16),
        jax.ShapeDtypeStruct((vision * KVH, HD), bf16),
    )
    found = pl.pallas_call(
        functools.partial(kernel, n_seq, n, pad, vision, group),
        out_shape=results[:2] + (jax.ShapeDtypeStruct((2, cols, 2 * HD), bf16),),
        in_specs=[hbm] * 5,
        out_specs=(hbm,) * 3,
        scratch_shapes=[
            pltpu.VMEM((tokens, width), bf16),
            pltpu.VMEM((tokens, width), bf16),
            pltpu.VMEM((tokens, width), bf16),
            pltpu.VMEM((tokens, width), bf16),
            pltpu.VMEM((vision * KVH, HD), bf16),
            pltpu.VMEM((vision * KVH, HD), bf16),
            pltpu.VMEM((2, tokens), mask.dtype),
            pltpu.VMEM((2, HD, heads * half), bf16),
            pltpu.VMEM((2, HD, heads * half), bf16),
            pltpu.VMEM((KVH * pad, 2 * HD), bf16),
            pltpu.VMEM((2, cols, 2 * HD), bf16),
            pltpu.VMEM((2, cols, 2 * HD), bf16),
            pltpu.VMEM((half, 2 * cols), f32),
            pltpu.VMEM((heads * half, 2 * cols), bf16),
            pltpu.VMEM((heads * half, cols), bf16),
            pltpu.VMEM((heads * half, 2 * cols), bf16),
            pltpu.VMEM((heads * half, cols), bf16),
            dma((2, 2)),
            dma((2, 2)),
            dma((3,)),
            dma((2, n)),
            dma((2, n)),
            dma((2, n)),
            dma((2, n)),
            dma,
        ],
        compiler_params=pltpu.CompilerParams(
            collective_id=0, has_side_effects=True, vmem_limit_bytes=VMEM_LIMIT
        ),
    )(
        queries,
        keys.reshape(vision * KVH, HD),
        values.reshape(vision * KVH, HD),
        cotangent,
        mask.T,
    )
    attended, grad_query, grad_keys, grad_values = pl.pallas_call(
        functools.partial(finish, n_seq, pad, vision),
        out_shape=results,
        in_specs=[hbm] * 3,
        out_specs=(hbm,) * 4,
        scratch_shapes=[
            pltpu.VMEM((tokens, width), bf16),
            pltpu.VMEM((tokens, width), bf16),
            pltpu.VMEM((2, cols, 2 * HD), bf16),
            pltpu.VMEM((vision * KVH, HD), bf16),
            pltpu.VMEM((vision * KVH, HD), bf16),
            dma((4,)),
            dma((4,)),
        ],
        compiler_params=pltpu.CompilerParams(vmem_limit_bytes=VMEM_LIMIT),
    )(*found)
    shape = (1, vision, KVH, HD)
    return attended, grad_query, grad_keys.reshape(shape), grad_values.reshape(shape)


def solution(mesh):
    return jax.shard_map(
        functools.partial(per_device, mesh.shape["seq"], mesh.shape["head"]),
        mesh=mesh,
        in_specs=(
            P("seq", "head"),
            P("seq", "head", None, None),
            P("seq", "head", None, None),
            P("seq", "head"),
            P("seq", None),
        ),
        out_specs=(
            P("seq", "head"),
            P("seq", "head"),
            P("seq", "head", None, None),
            P("seq", "head", None, None),
        ),
        check_vma=False,
    )
```

```python
import functools
import math

import jax
import jax.numpy as jnp
from jax import lax
from jax.experimental import pallas as pl
from jax.experimental.pallas import tpu as pltpu
from jax.sharding import PartitionSpec as P

KVH = 8
HD = 128
NEGATIVE = -1e30
VMEM_LIMIT = 58 * 1024 * 1024
MESH = pl.DeviceIdType.MESH
SCALE = HD ** -0.5
EXP2_SCALE = SCALE * math.log2(math.e)


def dot(a, b):
    return jnp.dot(a, b, preferred_element_type=jnp.float32)


def dot_nt(a, b):
    return lax.dot_general(a, b, (((1,), (1,)), ((), ())), preferred_element_type=jnp.float32)


def each(count, body):
    if count <= 8:
        for i in range(count):
            body(i)
    else:
        lax.fori_loop(0, count, lambda i, c: (body(i), c)[1], 0)


def slot_map(pad, vision, transposed):
    shape = (vision * KVH, KVH * pad) if transposed else (KVH * pad, vision * KVH)
    slot = lax.broadcasted_iota(jnp.int32, shape, 1 if transposed else 0)
    row = lax.broadcasted_iota(jnp.int32, shape, 0 if transposed else 1)
    head, token = slot // pad, slot % pad
    return jnp.where((token < vision) & (row == token * KVH + head), 1.0, 0.0).astype(jnp.bfloat16)


def kernel(
    n_seq, n, pad, vision, group,
    q_hbm, k_hbm, v_hbm, do_hbm, mask_hbm,
    att_hbm, gq_hbm, ret,
    q, do, att, gq, k_own, v_own, mask, qt, dot_t, stage, kv, part, bias, w_lower, w_upper, gs_lower, gs_upper,
    in_sem, out_sem, small_sem, kv_send, kv_recv, part_send, part_recv, kept_sem,
):
    s = lax.axis_index("seq")
    me = lax.axis_index("head")
    copies = n // KVH
    tokens, width = q.shape
    heads = width // HD
    half = tokens // 2
    cols = n * pad
    not_first = s > 0
    not_last = s < n_seq - 1

    small = []
    for i, (src, dst) in enumerate(((k_hbm, k_own), (v_hbm, v_own), (mask_hbm, mask))):
        load = pltpu.make_async_copy(src, dst, small_sem.at[i])
        load.start()
        small.append(load)
    loads = []
    for i, rows in enumerate((pl.ds(half, half), pl.ds(0, half))):
        for k, (src, dst) in enumerate(((q_hbm, q), (do_hbm, do))):
            load = pltpu.make_async_copy(src.at[rows], dst.at[rows], in_sem.at[i, k])
            load.start()
            loads.append(load)

    barrier = pltpu.get_barrier_semaphore()

    def greet(block, peer):
        pl.semaphore_signal(
            barrier, inc=1, device_id={"seq": block, "head": peer}, device_id_type=MESH
        )

    each(n - 1, lambda i: greet(s, lax.rem(me + 1 + i, n)))

    @pl.when(not_first)
    def _():
        each(n, lambda i: greet(s - 1, lax.rem(me + i, n)))

    @pl.when(not_last)
    def _():
        each(n, lambda i: greet(s + 1, lax.rem(me + i, n)))

    for load in small:
        load.wait()
    spread = slot_map(pad, vision, False)
    stage[:, :HD] = dot(spread, k_own[...]).astype(jnp.bfloat16)
    stage[:, HD:] = dot(spread, v_own[...]).astype(jnp.bfloat16)

    def rows_of(index):
        return pl.ds(pl.multiple_of(index * pad, pad), pad)

    def kv_copy(b, block, peer, source):
        return pltpu.make_async_remote_copy(
            src_ref=stage.at[rows_of(peer // copies)],
            dst_ref=kv.at[b, rows_of(source)],
            send_sem=kv_send.at[b, peer],
            recv_sem=kv_recv.at[b, source],
            device_id={"seq": block, "head": peer},
            device_id_type=MESH,
        )

    def part_copy(b, block, peer, source):
        return pltpu.make_async_remote_copy(
            src_ref=part.at[b, rows_of(peer)],
            dst_ref=ret.at[b, rows_of(source)],
            send_sem=part_send.at[b, peer],
            recv_sem=part_recv.at[b, source],
            device_id={"seq": block, "head": peer},
            device_id_type=MESH,
        )

    pl.semaphore_wait(
        barrier, (n - 1) + n * not_first.astype(jnp.int32) + n * not_last.astype(jnp.int32)
    )


    @pl.when(not_last)
    def _():
        each(n, lambda i: kv_copy(1, s + 1, lax.rem(me + i, n), me).start())

    each(n - 1, lambda i: kv_copy(0, s, lax.rem(me + 1 + i, n), me).start())
    kv[0, rows_of(me), :] = stage[rows_of(me // copies), :]

    @pl.when(s == 0)
    def _():
        kv[1] = jnp.zeros(kv.shape[1:], kv.dtype)

    slot_col = lax.broadcasted_iota(jnp.int32, (half, cols), 1)
    used = slot_col % pad < vision
    columns = jnp.concatenate(
        [jnp.broadcast_to(mask[i:i + 1, :half].astype(jnp.float32), (HD, half)) for i in range(2)],
        axis=0,
    ).T
    keep_own, keep_prev = columns[:, :1], columns[:, HD:HD + 1]
    bias[:, :cols] = jnp.where(used & (keep_own > 0), 0.0, NEGATIVE)
    bias[:, cols:] = jnp.where(used & (keep_prev > 0), 0.0, NEGATIVE)
    live = (keep_own + keep_prev > 0).astype(jnp.float32)
    live = jnp.concatenate([live] * group, axis=0)
    own_bias = jnp.where(used[:1], 0.0, NEGATIVE)

    for load in loads:
        load.wait()
    for h in range(heads):
        at = slice(h * HD, (h + 1) * HD)
        for b in range(2):
            to = slice(h * half, (h + 1) * half)
            rows = slice(b * half, (b + 1) * half)
            qt[b, :, to] = q[rows, at].T
            dot_t[b, :, to] = do[rows, at].T

    def stacked(ref, rows, first):
        return jnp.concatenate(
            [ref[rows, (first + i) * HD:(first + i + 1) * HD] for i in range(group)], axis=0
        )

    ones = jnp.ones((HD, HD), jnp.bfloat16)

    def attend(rows, first, keys, values, score_bias, live_rows, weight_store, grad_store):
        query = stacked(q, rows, first)
        grad = stacked(do, rows, first)
        tiles = keys.shape[0] // HD
        scores = dot_nt(query, keys) + score_bias
        yield
        grad_weights = dot_nt(grad, values)
        peak = jnp.max(scores, axis=1, keepdims=True)
        powered = jnp.exp2((scores - peak) * EXP2_SCALE)
        yield
        beside = jnp.concatenate([values, jnp.ones(values.shape, jnp.bfloat16)], axis=1)
        sums = dot(powered.astype(jnp.bfloat16), beside)
        ratio = live_rows / sums[:, HD:]
        attended = sums[:, :HD] * ratio
        delta = dot((grad.astype(jnp.float32) * attended).astype(jnp.bfloat16), ones)
        yield
        weights = powered * jnp.concatenate([ratio] * tiles, axis=1)
        grad_scores = weights * (grad_weights - jnp.concatenate([delta] * tiles, axis=1))
        for i in range(group):
            at = slice((first + i) * HD, (first + i + 1) * HD)
            att[rows, at] = attended[i * half:(i + 1) * half].astype(jnp.bfloat16)
        to = slice(first * half, (first + group) * half)
        weight_store[to, :] = weights.astype(jnp.bfloat16)
        grad_store[to, :] = grad_scores.astype(jnp.bfloat16)
        yield

    def in_step(chunks):
        stages = 4
        for time in range(stages + len(chunks) - 1):
            for place in reversed(range(len(chunks))):
                if 0 <= time - place < stages:
                    next(chunks[place])

    def put(b, key_sum, value_sum):
        part[b, :, :HD] = (key_sum * SCALE).T.astype(jnp.bfloat16)
        part[b, :, HD:] = value_sum.T.astype(jnp.bfloat16)

    def query_grads(rows, grad_store, keys):
        for first in firsts:
            grads = dot(grad_store[first * half:(first + group) * half, :], keys) * SCALE
            for i in range(group):
                at = slice((first + i) * HD, (first + i + 1) * HD)
                gq[rows, at] = grads[i * half:(i + 1) * half].astype(jnp.bfloat16)

    stores = []

    def write_out(src, dst, b, k):
        rows = pl.ds(b * half, half)
        store = pltpu.make_async_copy(src.at[rows], dst.at[rows], out_sem.at[b, k])
        store.start()
        stores.append(store)

    upper, lower = slice(half, tokens), slice(0, half)
    firsts = list(range(0, heads, group))

    each(n - 1, lambda i: kv_copy(0, s, me, lax.rem(me + 1 + i, n)).wait_recv())

    @pl.when(not_first)
    def _():
        each(n, lambda i: kv_copy(1, s, me, lax.rem(me + i, n)).wait_recv())

    both_keys = kv[:, :, :HD].reshape(2 * cols, HD)
    both_values = kv[:, :, HD:].reshape(2 * cols, HD)
    both_bias = jnp.concatenate([bias[...]] * group, axis=0)
    in_step([
        attend(lower, first, both_keys, both_values, both_bias, live, w_lower, gs_lower)
        for first in firsts
    ])
    put(1, dot(qt[0], gs_lower[:, cols:]), dot(dot_t[0], w_lower[:, cols:]))

    @pl.when(not_first)
    def _():
        each(n, lambda i: part_copy(1, s - 1, lax.rem(me + i, n), me).start())

    write_out(att, att_hbm, 0, 0)
    keys, values = kv[0, :, :HD], kv[0, :, HD:]
    in_step([
        attend(upper, first, keys, values, own_bias, 1.0, w_upper, gs_upper) for first in firsts
    ])
    put(
        0,
        dot(qt[0], gs_lower[:, :cols]) + dot(qt[1], gs_upper[...]),
        dot(dot_t[0], w_lower[:, :cols]) + dot(dot_t[1], w_upper[...]),
    )
    each(n - 1, lambda i: part_copy(0, s, lax.rem(me + 1 + i, n), me).start())
    kept = pltpu.make_async_copy(part.at[0, rows_of(me)], ret.at[0, rows_of(me)], kept_sem)
    kept.start()
    write_out(att, att_hbm, 1, 0)
    query_grads(upper, gs_upper, keys)
    write_out(gq, gq_hbm, 1, 1)
    query_grads(lower, gs_lower, both_keys)
    write_out(gq, gq_hbm, 0, 1)

    each(n - 1, lambda i: part_copy(0, s, me, lax.rem(me + 1 + i, n)).wait_recv())

    @pl.when(not_last)
    def _():
        each(n, lambda i: part_copy(1, s, me, lax.rem(me + i, n)).wait_recv())

    kept.wait()
    each(n - 1, lambda i: kv_copy(0, s, lax.rem(me + 1 + i, n), me).wait_send())
    each(n - 1, lambda i: part_copy(0, s, lax.rem(me + 1 + i, n), me).wait_send())

    @pl.when(not_last)
    def _():
        each(n, lambda i: kv_copy(1, s + 1, lax.rem(me + i, n), me).wait_send())

    @pl.when(not_first)
    def _():
        each(n, lambda i: part_copy(1, s - 1, lax.rem(me + i, n), me).wait_send())

    for store in stores:
        store.wait()


def finish(
    n_seq, pad, vision, att_in, gq_in, ret_in, att_out, gq_out, gk_out, gv_out,
    att, gq, ret, gk, gv, load_sem, store_sem,
):
    not_last = lax.axis_index("seq") < n_seq - 1
    own = pltpu.make_async_copy(ret_in.at[0], ret.at[0], load_sem.at[0])
    following = pltpu.make_async_copy(ret_in.at[1], ret.at[1], load_sem.at[1])
    own.start()
    pl.when(not_last)(following.start)
    loads, stores = [], []
    for i, (source, buffer, target) in enumerate(((att_in, att, att_out), (gq_in, gq, gq_out))):
        loads.append(pltpu.make_async_copy(source, buffer, load_sem.at[2 + i]))
        stores.append(pltpu.make_async_copy(buffer, target, store_sem.at[i]))
    for load in loads:
        load.start()

    @pl.when(jnp.logical_not(not_last))
    def _():
        ret[1] = jnp.zeros(ret.shape[1:], ret.dtype)

    gather = slot_map(pad, vision, True)
    own.wait()
    pl.when(not_last)(following.wait)
    for load, store in zip(loads, stores):
        load.wait()
        store.start()
    total = ret[0].astype(jnp.float32) + ret[1].astype(jnp.float32)
    copies = ret.shape[1] // (KVH * pad)
    total = total.reshape(KVH, copies, pad, 2 * HD).sum(axis=1).reshape(KVH * pad, 2 * HD)
    grads = dot(gather, total.astype(jnp.bfloat16)).astype(jnp.bfloat16)
    for i, (buffer, target) in enumerate(((gk, gk_out), (gv, gv_out))):
        buffer[...] = grads[:, i * HD:(i + 1) * HD]
        stores.append(pltpu.make_async_copy(buffer, target, store_sem.at[2 + i]))
        stores[-1].start()
    for store in stores:
        store.wait()


def per_device(n_seq, n, queries, keys, values, cotangent, mask):
    tokens, width = queries.shape
    vision = keys.shape[1]
    pad = -(-vision // 16) * 16
    heads = width // HD
    group = min(8, heads)
    half = tokens // 2
    cols = n * pad
    bf16, f32 = jnp.bfloat16, jnp.float32
    hbm = pl.BlockSpec(memory_space=pltpu.HBM)
    dma = pltpu.SemaphoreType.DMA
    results = (
        jax.ShapeDtypeStruct((tokens, width), bf16),
        jax.ShapeDtypeStruct((tokens, width), bf16),
        jax.ShapeDtypeStruct((vision * KVH, HD), bf16),
        jax.ShapeDtypeStruct((vision * KVH, HD), bf16),
    )
    found = pl.pallas_call(
        functools.partial(kernel, n_seq, n, pad, vision, group),
        out_shape=results[:2] + (jax.ShapeDtypeStruct((2, cols, 2 * HD), bf16),),
        in_specs=[hbm] * 5,
        out_specs=(hbm,) * 3,
        scratch_shapes=[
            pltpu.VMEM((tokens, width), bf16),
            pltpu.VMEM((tokens, width), bf16),
            pltpu.VMEM((tokens, width), bf16),
            pltpu.VMEM((tokens, width), bf16),
            pltpu.VMEM((vision * KVH, HD), bf16),
            pltpu.VMEM((vision * KVH, HD), bf16),
            pltpu.VMEM((2, tokens), mask.dtype),
            pltpu.VMEM((2, HD, heads * half), bf16),
            pltpu.VMEM((2, HD, heads * half), bf16),
            pltpu.VMEM((KVH * pad, 2 * HD), bf16),
            pltpu.VMEM((2, cols, 2 * HD), bf16),
            pltpu.VMEM((2, cols, 2 * HD), bf16),
            pltpu.VMEM((half, 2 * cols), f32),
            pltpu.VMEM((heads * half, 2 * cols), bf16),
            pltpu.VMEM((heads * half, cols), bf16),
            pltpu.VMEM((heads * half, 2 * cols), bf16),
            pltpu.VMEM((heads * half, cols), bf16),
            dma((2, 2)),
            dma((2, 2)),
            dma((3,)),
            dma((2, n)),
            dma((2, n)),
            dma((2, n)),
            dma((2, n)),
            dma,
        ],
        compiler_params=pltpu.CompilerParams(
            collective_id=0, has_side_effects=True, vmem_limit_bytes=VMEM_LIMIT
        ),
    )(
        queries,
        keys.reshape(vision * KVH, HD),
        values.reshape(vision * KVH, HD),
        cotangent,
        mask.T,
    )
    attended, grad_query, grad_keys, grad_values = pl.pallas_call(
        functools.partial(finish, n_seq, pad, vision),
        out_shape=results,
        in_specs=[hbm] * 3,
        out_specs=(hbm,) * 4,
        scratch_shapes=[
            pltpu.VMEM((tokens, width), bf16),
            pltpu.VMEM((tokens, width), bf16),
            pltpu.VMEM((2, cols, 2 * HD), bf16),
            pltpu.VMEM((vision * KVH, HD), bf16),
            pltpu.VMEM((vision * KVH, HD), bf16),
            dma((4,)),
            dma((4,)),
        ],
        compiler_params=pltpu.CompilerParams(vmem_limit_bytes=VMEM_LIMIT),
    )(*found)
    shape = (1, vision, KVH, HD)
    return attended, grad_query, grad_keys.reshape(shape), grad_values.reshape(shape)


def solution(mesh):
    return jax.shard_map(
        functools.partial(per_device, mesh.shape["seq"], mesh.shape["head"]),
        mesh=mesh,
        in_specs=(
            P("seq", "head"),
            P("seq", "head", None, None),
            P("seq", "head", None, None),
            P("seq", "head"),
            P("seq", None),
        ),
        out_specs=(
            P("seq", "head"),
            P("seq", "head"),
            P("seq", "head", None, None),
            P("seq", "head", None, None),
        ),
        check_vma=False,
    )
```
